32 devices in a mesh: groups: 2 (over x), graph: 4 (over y, core), chan: 4 (over z).
Axes of the slice: x: 2, y: 2, z: 4, core: 2. Of those that a mesh axis runs over, the one named last changes fastest.
Arguments:
- node_embed: bfloat16 [256, 2048], P(None, ('groups', 'graph')), parts along dimension 1, may hold values from -6 to 6
- edge_embed: bfloat16 [256, 16384], P(None, ('groups', 'graph')), parts along dimension 1, may hold values from -6 to 6
- edge_vector: float32 [3, 16384], P(None, ('groups', 'graph')), parts along dimension 1, may hold values from -6 to 6
- triplet_basis: bfloat16 [16, 65536], P(None, ('groups', 'graph')), parts along dimension 1, may hold values from -6 to 6
- w_source: bfloat16 [256, 256], P(None, 'chan'), may hold values from -0.375 to 0.375
- w_target: bfloat16 [256, 256], P(None, 'chan'), may hold values from -0.375 to 0.375
- w_edge: bfloat16 [256, 256], P(None, 'chan'), may hold values from -0.375 to 0.375
- w_radial: bfloat16 [128, 256], P(None, 'chan'), may hold values from -2 to 2
- w_angle: bfloat16 [16, 256], P(None, 'chan'), may hold values from -1.5 to 1.5
- w_energy: float32 [256], P('chan'), may hold values from -0.12 to 0.12
- node_send: int32 [8, 4, 64], P('groups'), parts along dimension 0, may hold values from -1 to 255, as said below
- edge_send: int32 [8, 4, 256], P('groups'), parts along dimension 0, may hold values from -1 to 2047, as said below
- edge_target: int32 [16384], P(('groups', 'graph')), parts along dimension 0, may hold values from 0 to 255
- edge_source: int32 [16384], P(('groups', 'graph')), parts along dimension 0, may hold values from 0 to 255, as said below
- triplet_in: int32 [65536], P(('groups', 'graph')), parts along dimension 0, may hold values from 0 to 1023, as said below
- triplet_out: int32 [65536], P(('groups', 'graph')), parts along dimension 0, may hold values from 0 to 2047
Outputs:
- node_out: bfloat16 [256, 2048], P('chan', ('groups', 'graph')), parts along dimension 1
- edge_out: bfloat16 [256, 16384], P('chan', ('groups', 'graph')), parts along dimension 1
- forces: float32 [3, 2048], P(None, ('groups', 'graph')), parts along dimension 1
The draws below stay inside these ranges and needn't reach their ends.
There are 2 independent parts, one for each index of `groups`. The reference program is written for one: setup_inputs(seed, part) draws one part's arguments, and reference() takes and returns one part's arrays. A program takes and returns all parts, laid end to end along the dimension named above; an argument that names none is the same for every part. Nothing has to cross between parts.
Inputs may be any that keep to these rules, and one draw needn't show every extreme that they name: node_send[q, p] lists distinct atoms of shard q (indices within that shard) sent to shard p: its first n entries, n from about 64 / 4 to 64, the rest -1. n = 64 when q = p, and for every q toward one shard p drawn anew. edge_send[q, p] lists distinct edges of shard q (indices within that shard) sent to shard p, laid out as node_send with 256 in place of 64. `edge_source`: each value is q * 64 + k where k is below the number of listed entries of node_send[q, p], p the edge's shard. `triplet_in`: each value is q * 256 + k where k is below the number of listed entries of edge_send[q, p], p the triplet's shard.
All inputs are finite; a program needn't handle non-finite values.
Results may differ from the reference program's by a relative error of at most 0.0075.
Values may be sent and summed in bfloat16 or wider, within the bound.
No kernel may reach another device: no remote copies, remote signals or barrier semaphores. Data moves between devices by JAX's collectives and lax.ppermute only.
A program may use at most 64 MiB of HBM per device.

```python
import jax
import jax.numpy as jnp
from jax import lax

D = 256
R = 128
S = 16
NODE_DEV = 256
EDGE_DEV = 2048
TRIP_DEV = 8192
CAP = 64
ECAP = 256
NODES = 1024
EDGES = 8192
TRIPS = 32768


def send_plan(key, salt, rows, capacity, peer_count):
    key = jax.random.fold_in(key, salt)
    first, second, third = jax.random.split(key, 3)
    scores = jax.random.randint(first, (peer_count, peer_count, rows), 0, 1 << 17)
    scores = scores * rows + jnp.arange(rows, dtype=jnp.int32)[None, None, :]
    chosen = jnp.argsort(scores, axis=-1)[:, :, :capacity].astype(jnp.int32)
    counts = jax.random.randint(second, (peer_count, peer_count), max(capacity // 4, 1), capacity + 1)
    fullest = jax.random.randint(third, (), 0, peer_count)
    sender = jnp.arange(peer_count)[:, None]
    receiver = jnp.arange(peer_count)[None, :]
    counts = jnp.where((sender == receiver) | (receiver == fullest), capacity, counts).astype(jnp.int32)
    slots = jnp.arange(capacity)[None, None, :]
    table = jnp.where(slots < counts[:, :, None], chosen, -1).astype(jnp.int32)
    return (table, counts)


def slot_draw(key, salt, rows, capacity, items, items_dev, peer_count):
    table, counts = send_plan(key, 11 + salt, rows, capacity, peer_count)
    key = jax.random.fold_in(key, 3 + salt)
    first, second = jax.random.split(key)
    owner = (jnp.arange(items) // items_dev).astype(jnp.int32)
    sender = jax.random.randint(first, (items,), 0, peer_count)
    pick = jax.random.randint(second, (items,), 0, 1 << 20) % counts[sender, owner]
    return (sender * capacity + pick).astype(jnp.int32)


def draw_node_send(key, part):
    table, counts = send_plan(key, 11, NODE_DEV, CAP, NODES // NODE_DEV)
    return table


def draw_edge_send(key, part):
    table, counts = send_plan(key, 12, EDGE_DEV, ECAP, NODES // NODE_DEV)
    return table


def draw_edge_source(key, part):
    return slot_draw(key, 0, NODE_DEV, CAP, EDGES, EDGE_DEV, NODES // NODE_DEV)


def draw_triplet_in(key, part):
    return slot_draw(key, 1, EDGE_DEV, ECAP, TRIPS, TRIP_DEV, NODES // NODE_DEV)


def touch_ends(entries, stream_key, least, high):
    place = [jax.random.randint(jax.random.fold_in(stream_key, axis), (), 0, length) for axis, length in enumerate(entries.shape)]
    widest = entries.shape.index(max(entries.shape))
    neighbour = place[:widest] + [(place[widest] + 1) % entries.shape[widest]] + place[widest + 1:]
    return entries.at[tuple(place)].set(least).at[tuple(neighbour)].set(high)


def levels(stream_key, dims, shards, least, high):
    def one(axis_at, blocks):
        heights = jax.random.uniform(jax.random.fold_in(jax.random.fold_in(stream_key, 6), axis_at), (blocks,), jnp.float32, least / len(shards), high / len(shards))
        return jnp.repeat(jnp.exp(heights), dims[axis_at] // blocks).reshape((-1,) + (1,) * (len(dims) - axis_at - 1))

    level = one(*shards[0])
    for cut in shards[1:]:
        level = level * one(*cut)
    return level


def bell_draw(stream_key, dims, scale, most, shards=(), kind=jnp.bfloat16):
    values = scale * jax.random.normal(stream_key, dims, jnp.float32)
    if shards:
        values = values * levels(stream_key, dims, shards, -0.22, 0.18)
    return jnp.clip(values, -most, most).astype(kind)


def setup_inputs(seed: int = 0, part: int = 0) -> dict:
    key_list = jax.random.split(jax.random.key(seed), 17)
    own_keys = jax.random.split(jax.random.fold_in(key_list[16], part), 17)
    node_embed = bell_draw(own_keys[0], (D, NODES), 1.0, 6.0, ((1, 4),))
    edge_embed = bell_draw(own_keys[1], (D, EDGES), 1.0, 6.0, ((1, 4),))
    edge_vector = bell_draw(own_keys[2], (3, EDGES), 1.5, 6.0, ((1, 4),), jnp.float32)
    triplet_basis = bell_draw(own_keys[3], (S, TRIPS), 1.0, 6.0, ((1, 4),))
    w_source = bell_draw(key_list[4], (D, D), D ** -0.5, 0.375, ((1, 4),))
    w_target = bell_draw(key_list[5], (D, D), D ** -0.5, 0.375, ((1, 4),))
    w_edge = bell_draw(key_list[6], (D, D), D ** -0.5, 0.375, ((1, 4),))
    w_radial = bell_draw(key_list[7], (R, D), (R // 16) ** -0.5, 2.0, ((1, 4),))
    w_angle = bell_draw(key_list[8], (S, D), S ** -0.5, 1.5, ((1, 4),))
    w_energy = bell_draw(key_list[9], (D,), 0.02, 0.12, ((0, 4),), jnp.float32)
    node_send = draw_node_send(jax.random.fold_in(jax.random.fold_in(key_list[16], part), 71), part)
    edge_send = draw_edge_send(jax.random.fold_in(jax.random.fold_in(key_list[16], part), 71), part)
    edge_target = touch_ends(jax.random.randint(own_keys[12], (EDGES,), 0, NODE_DEV), jax.random.fold_in(own_keys[12], 1), 0, NODE_DEV - 1).astype(jnp.int32)
    edge_source = draw_edge_source(jax.random.fold_in(jax.random.fold_in(key_list[16], part), 71), part)
    triplet_in = draw_triplet_in(jax.random.fold_in(jax.random.fold_in(key_list[16], part), 71), part)
    triplet_out = touch_ends(jax.random.randint(own_keys[15], (TRIPS,), 0, EDGE_DEV), jax.random.fold_in(own_keys[15], 1), 0, EDGE_DEV - 1).astype(jnp.int32)
    return dict(node_embed=node_embed, edge_embed=edge_embed, edge_vector=edge_vector, triplet_basis=triplet_basis, w_source=w_source, w_target=w_target, w_edge=w_edge, w_radial=w_radial, w_angle=w_angle, w_energy=w_energy, node_send=node_send, edge_send=edge_send, edge_target=edge_target, edge_source=edge_source, triplet_in=triplet_in, triplet_out=triplet_out)


radius_max = 8.0

def silu_slope(values):
    sig = jax.nn.sigmoid(values)
    return sig * (1.0 + values * (1.0 - sig))

def radial_terms(lengths):
    centers = jnp.arange(R).astype(jnp.float32) * (radius_max / (R - 1))
    spread = 4.0 * radius_max / (R - 1)
    offset = (lengths[None, :] - centers[:, None]) / spread
    values = jnp.exp(-offset * offset)
    slopes = values * (-2.0 * offset / spread)
    return (values.astype(jnp.bfloat16), slopes.astype(jnp.bfloat16))

def reference(node_embed, edge_embed, edge_vector, triplet_basis, w_source, w_target, w_edge, w_radial, w_angle, w_energy, node_send, edge_send, edge_target, edge_source, triplet_in, triplet_out):
    shard_count = NODES // NODE_DEV
    edge_shard = (jnp.arange(EDGES) // EDGE_DEV).astype(jnp.int32)
    src_peer = (edge_source // CAP).astype(jnp.int32)
    src_node = src_peer * NODE_DEV + node_send[src_peer, edge_shard, edge_source % CAP]
    dst_node = edge_shard * NODE_DEV + edge_target
    trip_shard = (jnp.arange(TRIPS) // TRIP_DEV).astype(jnp.int32)
    in_peer = (triplet_in // ECAP).astype(jnp.int32)
    in_edge = (in_peer * EDGE_DEV + edge_send[in_peer, trip_shard, triplet_in % ECAP]).astype(jnp.int32)
    out_edge = (trip_shard * EDGE_DEV + triplet_out).astype(jnp.int32)
    lengths = jnp.sqrt(1.0 + lax.optimization_barrier(jnp.sum(edge_vector * edge_vector, axis=0)))
    basis, slope = radial_terms(lengths)
    radial = jnp.dot(w_radial.T, basis, preferred_element_type=jnp.float32)
    radial_rate = jnp.dot(w_radial.T, slope, preferred_element_type=jnp.float32)
    proj_src = jnp.dot(w_source.T, node_embed, preferred_element_type=jnp.float32).astype(jnp.bfloat16)
    proj_dst = jnp.dot(w_target.T, node_embed, preferred_element_type=jnp.float32)
    proj_edge = jnp.dot(w_edge.T, edge_embed, preferred_element_type=jnp.float32)
    preact = proj_src[:, src_node].astype(jnp.float32) + proj_dst[:, dst_node] + proj_edge
    activated = jax.nn.silu(preact)
    message = (activated * radial).astype(jnp.bfloat16)
    basis_blocks = triplet_basis.reshape(S, shard_count, TRIP_DEV).transpose(1, 0, 2)
    in_blocks = in_edge.reshape(shard_count, TRIP_DEV)
    out_blocks = out_edge.reshape(shard_count, TRIP_DEV)

    def forward_block(total, block):
        basis_part, in_part, out_part = block
        angular = jnp.dot(w_angle.T, basis_part, preferred_element_type=jnp.float32)
        term = message[:, in_part].astype(jnp.float32) * angular
        return (total.at[:, out_part].add(term), None)
    gathered, unused = lax.scan(forward_block, jnp.zeros((D, EDGES), jnp.float32), (basis_blocks, in_blocks, out_blocks))
    edge_new = edge_embed.astype(jnp.float32) + message.astype(jnp.float32) + jax.nn.silu(gathered)
    edge_out = edge_new.astype(jnp.bfloat16)
    scale = (NODE_DEV / EDGE_DEV) ** 0.5
    node_new = node_embed.astype(jnp.float32) + scale * jnp.zeros((D, NODES), jnp.float32).at[:, dst_node].add(edge_new)
    node_out = node_new.astype(jnp.bfloat16)
    grad_node = w_energy[:, None] * silu_slope(node_new)
    grad_edge = scale * grad_node[:, dst_node]
    grad_gated = grad_edge * silu_slope(gathered)

    def backward_block(total, block):
        basis_part, in_part, out_part = block
        angular = jnp.dot(w_angle.T, basis_part, preferred_element_type=jnp.float32)
        term = grad_gated[:, out_part] * angular
        return (total.at[:, in_part].add(term), None)
    grad_msg, unused = lax.scan(backward_block, grad_edge, (basis_blocks, in_blocks, out_blocks))
    grad_len = lax.optimization_barrier(jnp.sum(grad_msg * activated * radial_rate, axis=0))
    push = grad_len[None, :] * edge_vector / lengths[None, :]
    at_target = jnp.zeros((3, NODES), jnp.float32).at[:, dst_node].add(push)
    at_source = jnp.zeros((3, NODES), jnp.float32).at[:, src_node].add(push)
    return (node_out, edge_out, at_source - at_target)
```

```python
import functools
import math

import jax
import jax.numpy as jnp
from jax import lax
from jax.experimental import pallas as pl
from jax.experimental.pallas import tpu as pltpu
from jax.sharding import PartitionSpec as P

NODE_DEV = 256
EDGE_DEV = 2048

radius_max = 8.0
MISC = 16
TERM = 8
BF = jnp.bfloat16
F32 = jnp.float32
VMEM_LIMIT = 40 * 1024 * 1024


def sigmoid(values):
    return 1.0 / (1.0 + jnp.exp(-values))


def dot_tn(weight, data):
    return lax.dot_general(weight, data, (((0,), (0,)), ((), ())), preferred_element_type=F32)


def dot_nn(left, right):
    return lax.dot_general(left, right, (((1,), (0,)), ((), ())), preferred_element_type=F32)


def dot_nt(left, right):
    return lax.dot_general(left, right, (((1,), (1,)), ((), ())), preferred_element_type=F32)


def one_hot(row, count):
    lines = lax.broadcasted_iota(jnp.int32, (count, row.shape[1]), 0)
    return jnp.where(lines == row, 1.0, 0.0).astype(BF)


def choose(stacked, group, groups):
    rows = stacked.shape[0] // groups
    out = jnp.where(group == 0, stacked[:rows], 0.0)
    for g in range(1, groups):
        out = jnp.where(group == g, stacked[g * rows : (g + 1) * rows], out)
    return out


def expand(values, group, groups):
    zero = jnp.zeros_like(values)
    return jnp.concatenate([jnp.where(group == g, values, zero) for g in range(groups)], axis=0)


def halves(values):
    high = values.astype(BF)
    return high, (values - high.astype(F32)).astype(BF)


def radial_terms(squared, weight):
    count = weight.shape[0]
    lengths = jnp.sqrt(1.0 + squared)
    spread = 4.0 * radius_max / (count - 1)
    lines = lax.broadcasted_iota(jnp.int32, (count, 1), 0).astype(F32)
    centers = lines * (radius_max / (count - 1))
    offset = (lengths - centers) * (1.0 / spread)
    values = jnp.exp(-offset * offset)
    slopes = values * (offset * (-2.0 / spread))
    return dot_tn(weight, values.astype(BF)), dot_tn(weight, slopes.astype(BF)), lengths


def squared_length(vector):
    return vector[0:1] * vector[0:1] + vector[1:2] * vector[1:2] + vector[2:3] * vector[2:3]


def prep_kernel(
    node, edge, vector, w_source, w_target, w_edge, node_send, edge_send, target, source, part_out, misc_out, *sends
):
    me = lax.axis_index("graph")
    peers = len(sends)
    channels = w_source.shape[1]
    edges = edge.shape[1]
    cap = node_send.shape[2]
    high_count = 4
    low_count = edges // high_count
    atoms = node[...]
    proj_src = dot_tn(w_source[...], atoms).astype(BF)
    dst_high, dst_low = halves(dot_tn(w_target[...], atoms))
    dst_table = jnp.concatenate([dst_high, dst_low], axis=0)
    own_nodes = jnp.concatenate([node_send[q, pl.ds(me, 1), :] for q in range(peers)], axis=0)
    own_nodes = own_nodes.astype(F32).astype(BF)
    parts = []
    for h in range(high_count):
        cols = slice(h * low_count, (h + 1) * low_count)
        dst = target[:, cols]
        src = source[:, cols]
        rows = dot_nn(dst_table, one_hot(dst, atoms.shape[1]))
        part = rows[:channels] + rows[channels:] + dot_tn(w_edge[...], edge[:, cols])
        part_out[:, cols] = part
        src_peer = src // cap
        by_peer = dot_nn(own_nodes, one_hot(src - src_peer * cap, cap))
        src_node = choose(by_peer, src_peer, peers)
        vec = vector[:, cols]
        first = vec.astype(BF).astype(F32)
        second = (vec - first).astype(BF).astype(F32)
        third = vec - first - second
        misc = jnp.concatenate(
            [
                first,
                second,
                third,
                dst.astype(F32),
                src_node,
                src_peer.astype(F32),
                jnp.zeros((MISC - 12, low_count), F32),
            ],
            axis=0,
        )
        misc_out[:, cols] = misc
        parts.append(jnp.concatenate([part.astype(BF), misc.astype(BF)], axis=0))
    table = jnp.concatenate(parts, axis=0)
    for d in range(peers):
        chosen = edge_send[me, pl.ds(jnp.bitwise_xor(me, d), 1), :]
        high = jnp.where(chosen < 0, -1, chosen // low_count)
        picked = choose(dot_nn(table, one_hot(chosen % low_count, low_count)), high, high_count)
        sends[d][:channels] = proj_src
        sends[d][channels:] = picked.astype(BF)


def local_kernel(vector, w_radial, radial_out, rate_out):
    edges = vector.shape[1]
    width = min(512, edges)
    for start in range(0, edges, width):
        cols = slice(start, start + width)
        radial, rate, _ = radial_terms(squared_length(vector[:, cols]), w_radial[...])
        radial_out[:, cols] = radial
        rate_out[:, cols] = rate


def main_kernel(
    peers,
    ecap,
    scale,
    part,
    misc,
    radial,
    rate,
    vector,
    node,
    edge,
    basis,
    w_radial,
    w_angle,
    w_energy,
    trip_in,
    trip_out,
    target,
    *refs,
):
    received = refs[:peers]
    node_out, edge_out, force_out = refs[peers : peers + 3]
    message, own_rate, slot_rate, slot_table, angular, gather_sum, grad_table, edge_grad, slot_sum, moves = refs[peers + 3 :]
    me = lax.axis_index("graph")
    channels, edges = part.shape
    nodes = node.shape[1]
    trips = basis.shape[1]
    first_chan = pl.multiple_of(lax.axis_index("chan") * channels, channels)
    groups = slot_table.shape[0] // channels
    low_in = slot_table.shape[1]
    low_out = edges // groups
    step = 512
    width = 256

    src_table = jnp.concatenate([received[d][:channels] for d in range(peers)], axis=0)

    def src_rows(src_node, src_peer):
        rows = dot_nn(src_table, one_hot(src_node, nodes))
        return choose(rows, jnp.bitwise_xor(src_peer, me), peers)

    for start in range(0, edges, step):
        cols = slice(start, start + step)
        rows = src_rows(misc[10:11, cols].astype(jnp.int32), misc[11:12, cols].astype(jnp.int32))
        preact = rows + part[:, cols]
        active = preact * sigmoid(preact)
        message[:, cols] = (active * radial[:, cols]).astype(BF)
        own_rate[:, cols] = active * rate[:, cols]
    slots = []
    for d in range(peers):
        cols = slice(d * ecap, (d + 1) * ecap)
        extra = received[d][channels:].astype(F32)
        rest = extra[channels:]
        vec = rest[0:3] + rest[3:6] + rest[6:9]
        src_node = rest[10:11].astype(jnp.int32)
        src_peer = rest[11:12].astype(jnp.int32)
        slot_radial, slot_slope, lengths = radial_terms(squared_length(vec), w_radial[...])
        preact = src_rows(src_node, src_peer) + extra[:channels]
        active = preact * sigmoid(preact)
        place = d * ecap
        low = place % low_in
        slot_table[(place // low_in) * channels : (place // low_in + 1) * channels, low : low + ecap] = (
            active * slot_radial
        ).astype(BF)
        slot_rate[:, cols] = active * slot_slope
        slots.append((vec / lengths, src_node, src_peer, rest[9:10].astype(jnp.int32)))

    def split_in(cols):
        place = jnp.bitwise_xor(trip_in[:, cols], me * ecap)
        high = place // low_in
        return high, one_hot(place - high * low_in, low_in)

    def split_out(cols):
        place = trip_out[:, cols]
        high = place // low_out
        return high, one_hot(place - high * low_out, low_out)

    gather_sum[...] = jnp.zeros_like(gather_sum)
    weight = w_angle[...]

    def forward(turn, carry):
        total = None
        for sub in range(step // width):
            cols = pl.ds(pl.multiple_of(turn * step + sub * width, width), width)
            high_in, hot_in = split_in(cols)
            high_out, hot_out = split_out(cols)
            angle = dot_tn(weight, basis[:, cols])
            angular[:, cols] = angle
            term = (choose(dot_nn(slot_table[...], hot_in), high_in, groups) * angle).astype(BF)
            more = dot_nt(hot_out, expand(term, high_out, groups))
            total = more if total is None else total + more
        gather_sum[...] += total
        return carry

    lax.fori_loop(0, trips // step, forward, 0)

    gathered = gather_sum[...].T
    atom_sum = jnp.zeros((channels, nodes), F32)
    for g in range(groups):
        cols = slice(g * low_out, (g + 1) * low_out)
        value = gathered[g * channels : (g + 1) * channels]
        own_edge = edge[pl.ds(first_chan, channels), cols].astype(F32)
        fresh = own_edge + message[:, cols].astype(F32) + value * sigmoid(value)
        edge_out[:, cols] = fresh.astype(BF)
        high, low = halves(fresh)
        sums = dot_nt(jnp.concatenate([high, low], axis=0), one_hot(target[:, cols], nodes))
        atom_sum += sums[:channels] + sums[channels:]
    node_new = node[pl.ds(first_chan, channels), :].astype(F32) + scale * atom_sum
    node_out[...] = node_new.astype(BF)
    sig = sigmoid(node_new)
    grad_node = w_energy[...] * (sig * (1.0 + node_new * (1.0 - sig))) * scale
    high, low = halves(grad_node)
    grad_pair = jnp.concatenate([high, low], axis=0)
    pushes = []
    for g in range(groups):
        cols = slice(g * low_out, (g + 1) * low_out)
        value = gathered[g * channels : (g + 1) * channels]
        rows = dot_nn(grad_pair, one_hot(target[:, cols], nodes))
        grad_edge = rows[:channels] + rows[channels:]
        sig = sigmoid(value)
        grad_table[g * channels : (g + 1) * channels, :] = (
            grad_edge * (sig * (1.0 + value * (1.0 - sig)))
        ).astype(BF)
        edge_grad[:, cols] = jnp.sum(grad_edge * own_rate[:, cols], axis=0, keepdims=True)

    slot_sum[...] = jnp.zeros_like(slot_sum)

    def backward(turn, carry):
        total = None
        for sub in range(step // width):
            cols = pl.ds(pl.multiple_of(turn * step + sub * width, width), width)
            high_in, hot_in = split_in(cols)
            high_out, hot_out = split_out(cols)
            term = (choose(dot_nn(grad_table[...], hot_out), high_out, groups) * angular[:, cols]).astype(BF)
            more = dot_nt(hot_in, expand(term, high_in, groups))
            total = more if total is None else total + more
        slot_sum[...] += total
        return carry

    lax.fori_loop(0, trips // step, backward, 0)

    moves[...] = jnp.zeros_like(moves)

    def push_terms(push):
        high = push.astype(BF).astype(F32)
        return jnp.concatenate([high, push - high, jnp.zeros((TERM - 6, push.shape[1]), F32)], axis=0)

    for start in range(0, edges, step):
        cols = slice(start, start + step)
        vec = vector[:, cols]
        terms = push_terms(vec * (edge_grad[:, cols] / jnp.sqrt(1.0 + squared_length(vec))))
        src_peer = jnp.bitwise_xor(misc[11:12, cols].astype(jnp.int32), me)
        moves[...] += dot_nt(
            expand(terms, src_peer, peers).astype(BF), one_hot(misc[10:11, cols].astype(jnp.int32), nodes)
        )
        moves[:TERM] -= dot_nt(
            jnp.concatenate([terms, jnp.zeros_like(terms)], axis=0).astype(BF), one_hot(target[:, cols], nodes)
        )[:TERM]
    slot_grad = slot_sum[...].T
    for d in range(peers):
        cols = slice(d * ecap, (d + 1) * ecap)
        place = d * ecap
        low = place % low_in
        grads = slot_grad[(place // low_in) * channels : (place // low_in + 1) * channels, low : low + ecap]
        unit, src_node, src_peer, dst_node = slots[d]
        terms = push_terms(unit * jnp.sum(grads * slot_rate[:, cols], axis=0, keepdims=True))
        moves[...] += dot_nt(
            expand(terms, jnp.bitwise_xor(src_peer, me), peers).astype(BF), one_hot(src_node, nodes)
        )
        moves[d * TERM : (d + 1) * TERM] -= dot_nt(
            jnp.concatenate([terms, jnp.zeros_like(terms)], axis=0).astype(BF), one_hot(dst_node, nodes)
        )[:TERM]
    force_out[...] = moves[...].reshape(force_out.shape)


def exchange(values, axis, distance):
    count = lax.axis_size(axis)
    return lax.ppermute(values, axis, [(i, i ^ distance) for i in range(count)])


def add_over(values, axis):
    count = lax.axis_size(axis)
    if count <= 4:
        others = [exchange(values, axis, d) for d in range(1, count)]
        return functools.reduce(jnp.add, others, values)
    for bit in range(count.bit_length() - 1):
        values = values + exchange(values, axis, 1 << bit)
    return values


def shards(
    node_embed,
    edge_embed,
    edge_vector,
    triplet_basis,
    w_source,
    w_target,
    w_edge,
    w_radial,
    w_angle,
    w_energy,
    node_send,
    edge_send,
    edge_target,
    edge_source,
    triplet_in,
    triplet_out,
):
    peers = lax.axis_size("graph")
    channels = w_source.shape[1]
    nodes = node_embed.shape[1]
    edges = edge_embed.shape[1]
    trips = triplet_basis.shape[1]
    ecap = edge_send.shape[2]
    groups = 256 // channels
    low_in = peers * ecap // groups
    low_out = edges // groups
    target = edge_target.reshape(1, edges)
    source = edge_source.reshape(1, edges)
    params = pltpu.CompilerParams(vmem_limit_bytes=VMEM_LIMIT)
    part, misc, *sends = pl.pallas_call(
        prep_kernel,
        name="prep",
        out_shape=[
            jax.ShapeDtypeStruct((channels, edges), F32),
            jax.ShapeDtypeStruct((MISC, edges), F32),
        ]
        + [jax.ShapeDtypeStruct((2 * channels + MISC, ecap), BF)] * peers,
        compiler_params=params,
    )(node_embed, edge_embed, edge_vector, w_source, w_target, w_edge, node_send, edge_send, target, source)
    received = [sends[0]] + [exchange(sends[d], "graph", d) for d in range(1, peers)]
    radial, rate = pl.pallas_call(
        local_kernel,
        name="local",
        out_shape=[jax.ShapeDtypeStruct((channels, edges), F32)] * 2,
        compiler_params=params,
        cost_estimate=pl.CostEstimate(flops=2**28, bytes_accessed=2**21, transcendentals=2**18),
    )(edge_vector, w_radial)
    node_out, edge_out, force = pl.pallas_call(
        functools.partial(main_kernel, peers, ecap, math.sqrt(NODE_DEV / EDGE_DEV)),
        name="main",
        out_shape=[
            jax.ShapeDtypeStruct((channels, nodes), BF),
            jax.ShapeDtypeStruct((channels, edges), BF),
            jax.ShapeDtypeStruct((peers, TERM, nodes), F32),
        ],
        scratch_shapes=[
            pltpu.VMEM((channels, edges), BF),
            pltpu.VMEM((channels, edges), F32),
            pltpu.VMEM((channels, peers * ecap), F32),
            pltpu.VMEM((groups * channels, low_in), BF),
            pltpu.VMEM((channels, trips), F32),
            pltpu.VMEM((low_out, groups * channels), F32),
            pltpu.VMEM((groups * channels, low_out), BF),
            pltpu.VMEM((1, edges), F32),
            pltpu.VMEM((low_in, groups * channels), F32),
            pltpu.VMEM((peers * TERM, nodes), F32),
        ],
        compiler_params=params,
    )(
        part,
        misc,
        radial,
        rate,
        edge_vector,
        node_embed,
        edge_embed,
        triplet_basis,
        w_radial,
        w_angle,
        w_energy.reshape(channels, 1),
        triplet_in.reshape(1, trips),
        triplet_out.reshape(1, trips),
        target,
        *received,
    )
    mine = force[0]
    for d in range(1, peers):
        mine = mine + exchange(force[d], "graph", d)
    mine = add_over(mine, "chan")
    return node_out, edge_out, mine[0:3] + mine[3:6]


def solution(mesh):
    placed = (
        P(None, ("groups", "graph")),
        P(None, ("groups", "graph")),
        P(None, ("groups", "graph")),
        P(None, ("groups", "graph")),
        P(None, "chan"),
        P(None, "chan"),
        P(None, "chan"),
        P(None, "chan"),
        P(None, "chan"),
        P("chan"),
        P("groups", None, None),
        P("groups", None, None),
        P(("groups", "graph")),
        P(("groups", "graph")),
        P(("groups", "graph")),
        P(("groups", "graph")),
    )
    return jax.shard_map(
        shards,
        mesh=mesh,
        in_specs=placed,
        out_specs=(
            P("chan", ("groups", "graph")),
            P("chan", ("groups", "graph")),
            P(None, ("groups", "graph")),
        ),
        check_vma=False,
    )
```

```python
import functools
import math

import jax
import jax.numpy as jnp
from jax import lax
from jax.experimental import pallas as pl
from jax.experimental.pallas import tpu as pltpu
from jax.sharding import PartitionSpec as P

NODE_DEV = 256
EDGE_DEV = 2048

radius_max = 8.0
MISC = 16
TERM = 8
BF = jnp.bfloat16
F32 = jnp.float32
VMEM_LIMIT = 40 * 1024 * 1024


def sigmoid(values):
    return 1.0 / (1.0 + jnp.exp(-values))


def dot_tn(weight, data):
    return lax.dot_general(weight, data, (((0,), (0,)), ((), ())), preferred_element_type=F32)


def dot_nn(left, right):
    return lax.dot_general(left, right, (((1,), (0,)), ((), ())), preferred_element_type=F32)


def dot_nt(left, right):
    return lax.dot_general(left, right, (((1,), (1,)), ((), ())), preferred_element_type=F32)


def one_hot(row, count):
    lines = lax.broadcasted_iota(jnp.int32, (count, row.shape[1]), 0)
    return jnp.where(lines == row, 1.0, 0.0).astype(BF)


def choose(stacked, group, groups):
    rows = stacked.shape[0] // groups
    out = jnp.where(group == 0, stacked[:rows], 0.0)
    for g in range(1, groups):
        out = jnp.where(group == g, stacked[g * rows : (g + 1) * rows], out)
    return out


def expand(values, group, groups):
    zero = jnp.zeros_like(values)
    return jnp.concatenate([jnp.where(group == g, values, zero) for g in range(groups)], axis=0)


def halves(values):
    high = values.astype(BF)
    return high, (values - high.astype(F32)).astype(BF)


def radial_terms(squared, weight):
    count = weight.shape[1]
    lengths = jnp.sqrt(1.0 + squared)
    spread = 4.0 * radius_max / (count - 1)
    lines = lax.broadcasted_iota(jnp.int32, (count, 1), 0).astype(F32)
    centers = lines * (radius_max / (count - 1))
    offset = (lengths - centers) * (1.0 / spread)
    values = jnp.exp(-offset * offset)
    slopes = values * (offset * (-2.0 / spread))
    return dot_nn(weight, values.astype(BF)), dot_nn(weight, slopes.astype(BF)), lengths


def squared_length(vector):
    return vector[0:1] * vector[0:1] + vector[1:2] * vector[1:2] + vector[2:3] * vector[2:3]


def prep_kernel(
    node,
    edge,
    vector,
    w_source,
    w_target,
    w_edge,
    node_send,
    edge_send,
    target,
    source,
    part_out,
    misc_out,
    own_node_out,
    own_edge_out,
    *sends,
):
    me = lax.axis_index("graph")
    peers = len(sends)
    channels = w_source.shape[0]
    first_chan = pl.multiple_of(lax.axis_index("chan") * channels, channels)
    edges = edge.shape[1]
    cap = node_send.shape[2]
    high_count = 4
    low_count = edges // high_count
    atoms = node[...]
    own_node_out[...] = node[pl.ds(first_chan, channels), :]
    own_edge_out[...] = edge[pl.ds(first_chan, channels), :]
    proj_src = dot_nn(w_source[...], atoms).astype(BF)
    dst_high, dst_low = halves(dot_nn(w_target[...], atoms))
    dst_table = jnp.concatenate([dst_high, dst_low], axis=0)
    own_nodes = jnp.concatenate([node_send[q, pl.ds(me, 1), :] for q in range(peers)], axis=0)
    own_nodes = own_nodes.astype(F32).astype(BF)
    parts = []
    for h in range(high_count):
        cols = slice(h * low_count, (h + 1) * low_count)
        dst = target[:, cols]
        src = source[:, cols]
        rows = dot_nn(dst_table, one_hot(dst, atoms.shape[1]))
        part = rows[:channels] + rows[channels:] + dot_nn(w_edge[...], edge[:, cols])
        part_out[:, cols] = part
        src_peer = src // cap
        by_peer = dot_nn(own_nodes, one_hot(src - src_peer * cap, cap))
        src_node = choose(by_peer, src_peer, peers)
        vec = vector[:, cols]
        first = vec.astype(BF).astype(F32)
        second = (vec - first).astype(BF).astype(F32)
        third = vec - first - second
        misc = jnp.concatenate(
            [
                first,
                second,
                third,
                dst.astype(F32),
                src_node,
                src_peer.astype(F32),
                jnp.zeros((MISC - 12, low_count), F32),
            ],
            axis=0,
        )
        misc_out[:, cols] = misc
        parts.append(jnp.concatenate([part.astype(BF), misc.astype(BF)], axis=0))
    table = jnp.concatenate(parts, axis=0)
    for d in range(peers):
        chosen = edge_send[me, pl.ds(jnp.bitwise_xor(me, d), 1), :]
        high = jnp.where(chosen < 0, -1, chosen // low_count)
        picked = choose(dot_nn(table, one_hot(chosen % low_count, low_count)), high, high_count)
        sends[d][:channels] = proj_src
        sends[d][channels:] = picked.astype(BF)


def local_kernel(vector, w_radial, radial_out, rate_out):
    edges = vector.shape[1]
    width = min(512, edges)
    for start in range(0, edges, width):
        cols = slice(start, start + width)
        radial, rate, _ = radial_terms(squared_length(vector[:, cols]), w_radial[...])
        radial_out[:, cols] = radial
        rate_out[:, cols] = rate


def main_kernel(
    peers,
    ecap,
    scale,
    part,
    misc,
    radial,
    rate,
    vector,
    node,
    edge,
    basis,
    w_radial,
    w_angle,
    w_energy,
    trip_in,
    trip_out,
    target,
    *refs,
):
    received = refs[:peers]
    node_out, edge_out, force_out = refs[peers : peers + 3]
    message, own_rate, slot_rate, slot_table, angular, gather_sum, grad_table, edge_grad, slot_sum, moves = refs[peers + 3 :]
    me = lax.axis_index("graph")
    channels, edges = part.shape
    nodes = node.shape[1]
    trips = basis.shape[1]
    groups = slot_table.shape[0] // channels
    low_in = slot_table.shape[1]
    low_out = edges // groups
    step = 512
    width = min(1024, trips)
    turn_width = min(4096, trips)

    src_table = jnp.concatenate([received[d][:channels] for d in range(peers)], axis=0)

    def src_rows(src_node, src_peer):
        rows = dot_nn(src_table, one_hot(src_node, nodes))
        return choose(rows, jnp.bitwise_xor(src_peer, me), peers)

    for start in range(0, edges, step):
        cols = slice(start, start + step)
        rows = src_rows(misc[10:11, cols].astype(jnp.int32), misc[11:12, cols].astype(jnp.int32))
        preact = rows + part[:, cols]
        active = preact * sigmoid(preact)
        message[:, cols] = (active * radial[:, cols]).astype(BF)
        own_rate[:, cols] = active * rate[:, cols]
    slots = []
    for d in range(peers):
        cols = slice(d * ecap, (d + 1) * ecap)
        extra = received[d][channels:].astype(F32)
        rest = extra[channels:]
        vec = rest[0:3] + rest[3:6] + rest[6:9]
        src_node = rest[10:11].astype(jnp.int32)
        src_peer = rest[11:12].astype(jnp.int32)
        slot_radial, slot_slope, lengths = radial_terms(squared_length(vec), w_radial[...])
        preact = src_rows(src_node, src_peer) + extra[:channels]
        active = preact * sigmoid(preact)
        place = d * ecap
        low = place % low_in
        slot_table[(place // low_in) * channels : (place // low_in + 1) * channels, low : low + ecap] = (
            active * slot_radial
        ).astype(BF)
        slot_rate[:, cols] = active * slot_slope
        slots.append((vec / lengths, src_node, src_peer, rest[9:10].astype(jnp.int32)))

    def split_in(cols):
        place = jnp.bitwise_xor(trip_in[:, cols], me * ecap)
        high = place // low_in
        return high, one_hot(place - high * low_in, low_in)

    def split_out(cols):
        place = trip_out[:, cols]
        high = place // low_out
        return high, one_hot(place - high * low_out, low_out)

    gather_sum[...] = jnp.zeros_like(gather_sum)
    weight = w_angle[...]

    def forward(turn, carry):
        total = None
        for sub in range(turn_width // width):
            cols = pl.ds(pl.multiple_of(turn * turn_width + sub * width, width), width)
            high_in, hot_in = split_in(cols)
            high_out, hot_out = split_out(cols)
            angle = dot_tn(weight, basis[:, cols])
            angular[:, cols] = angle
            term = (choose(dot_nn(slot_table[...], hot_in), high_in, groups) * angle).astype(BF)
            more = dot_nt(hot_out, expand(term, high_out, groups))
            total = more if total is None else total + more
        gather_sum[...] += total
        return carry

    lax.fori_loop(0, trips // turn_width, forward, 0)

    gathered = gather_sum[...].T
    atom_sum = jnp.zeros((channels, nodes), F32)
    for g in range(groups):
        cols = slice(g * low_out, (g + 1) * low_out)
        value = gathered[g * channels : (g + 1) * channels]
        own_edge = edge[:, cols].astype(F32)
        fresh = own_edge + message[:, cols].astype(F32) + value * sigmoid(value)
        edge_out[:, cols] = fresh.astype(BF)
        high, low = halves(fresh)
        sums = dot_nt(jnp.concatenate([high, low], axis=0), one_hot(target[:, cols], nodes))
        atom_sum += sums[:channels] + sums[channels:]
    lines = lax.broadcasted_iota(jnp.int32, (channels, channels), 0)
    diagonal = lines == lax.broadcasted_iota(jnp.int32, (channels, channels), 1)
    energy = jnp.sum(jnp.where(diagonal, w_energy[...], 0.0), axis=1, keepdims=True)
    node_new = node[...].astype(F32) + scale * atom_sum
    node_out[...] = node_new.astype(BF)
    sig = sigmoid(node_new)
    grad_node = energy * (sig * (1.0 + node_new * (1.0 - sig))) * scale
    high, low = halves(grad_node)
    grad_pair = jnp.concatenate([high, low], axis=0)
    pushes = []
    for g in range(groups):
        cols = slice(g * low_out, (g + 1) * low_out)
        value = gathered[g * channels : (g + 1) * channels]
        rows = dot_nn(grad_pair, one_hot(target[:, cols], nodes))
        grad_edge = rows[:channels] + rows[channels:]
        sig = sigmoid(value)
        grad_table[g * channels : (g + 1) * channels, :] = (
            grad_edge * (sig * (1.0 + value * (1.0 - sig)))
        ).astype(BF)
        edge_grad[:, cols] = jnp.sum(grad_edge * own_rate[:, cols], axis=0, keepdims=True)

    slot_sum[...] = jnp.zeros_like(slot_sum)

    def backward(turn, carry):
        total = None
        for sub in range(turn_width // width):
            cols = pl.ds(pl.multiple_of(turn * turn_width + sub * width, width), width)
            high_in, hot_in = split_in(cols)
            high_out, hot_out = split_out(cols)
            term = (choose(dot_nn(grad_table[...], hot_out), high_out, groups) * angular[:, cols]).astype(BF)
            more = dot_nt(hot_in, expand(term, high_in, groups))
            total = more if total is None else total + more
        slot_sum[...] += total
        return carry

    lax.fori_loop(0, trips // turn_width, backward, 0)

    moves[...] = jnp.zeros_like(moves)

    def push_terms(push):
        high = push.astype(BF).astype(F32)
        return jnp.concatenate([high, push - high, jnp.zeros((TERM - 6, push.shape[1]), F32)], axis=0)

    for start in range(0, edges, step):
        cols = slice(start, start + step)
        vec = vector[:, cols]
        terms = push_terms(vec * (edge_grad[:, cols] / jnp.sqrt(1.0 + squared_length(vec))))
        src_peer = jnp.bitwise_xor(misc[11:12, cols].astype(jnp.int32), me)
        moves[...] += dot_nt(
            expand(terms, src_peer, peers).astype(BF), one_hot(misc[10:11, cols].astype(jnp.int32), nodes)
        )
        moves[:TERM] -= dot_nt(
            jnp.concatenate([terms, jnp.zeros_like(terms)], axis=0).astype(BF), one_hot(target[:, cols], nodes)
        )[:TERM]
    slot_grad = slot_sum[...].T
    for d in range(peers):
        cols = slice(d * ecap, (d + 1) * ecap)
        place = d * ecap
        low = place % low_in
        grads = slot_grad[(place // low_in) * channels : (place // low_in + 1) * channels, low : low + ecap]
        unit, src_node, src_peer, dst_node = slots[d]
        terms = push_terms(unit * jnp.sum(grads * slot_rate[:, cols], axis=0, keepdims=True))
        moves[...] += dot_nt(
            expand(terms, jnp.bitwise_xor(src_peer, me), peers).astype(BF), one_hot(src_node, nodes)
        )
        moves[d * TERM : (d + 1) * TERM] -= dot_nt(
            jnp.concatenate([terms, jnp.zeros_like(terms)], axis=0).astype(BF), one_hot(dst_node, nodes)
        )[:TERM]
    force_out[...] = moves[...].reshape(force_out.shape)


def exchange(values, axis, distance):
    count = lax.axis_size(axis)
    return lax.ppermute(values, axis, [(i, i ^ distance) for i in range(count)])


def add_over(values, axis):
    count = lax.axis_size(axis)
    if count <= 4:
        others = [exchange(values, axis, d) for d in range(1, count)]
        return functools.reduce(jnp.add, others, values)
    for bit in range(count.bit_length() - 1):
        values = values + exchange(values, axis, 1 << bit)
    return values


def shards(
    node_embed,
    edge_embed,
    edge_vector,
    triplet_basis,
    w_source,
    w_target,
    w_edge,
    w_radial,
    w_angle,
    w_energy,
    node_send,
    edge_send,
    edge_target,
    edge_source,
    triplet_in,
    triplet_out,
):
    peers = lax.axis_size("graph")
    channels = w_source.shape[1]
    nodes = node_embed.shape[1]
    edges = edge_embed.shape[1]
    trips = triplet_basis.shape[1]
    ecap = edge_send.shape[2]
    groups = 256 // channels
    low_in = peers * ecap // groups
    low_out = edges // groups
    target = edge_target.reshape(1, edges)
    source = edge_source.reshape(1, edges)
    params = pltpu.CompilerParams(vmem_limit_bytes=VMEM_LIMIT)
    part, misc, own_node, own_edge, *sends = pl.pallas_call(
        prep_kernel,
        name="prep",
        out_shape=[
            jax.ShapeDtypeStruct((channels, edges), F32),
            jax.ShapeDtypeStruct((MISC, edges), F32),
            jax.ShapeDtypeStruct((channels, nodes), BF),
            jax.ShapeDtypeStruct((channels, edges), BF),
        ]
        + [jax.ShapeDtypeStruct((2 * channels + MISC, ecap), BF)] * peers,
        compiler_params=params,
    )(node_embed, edge_embed, edge_vector, w_source.T, w_target.T, w_edge.T, node_send, edge_send, target, source)
    received = [sends[0]] + [exchange(sends[d], "graph", d) for d in range(1, peers)]
    radial, rate = pl.pallas_call(
        local_kernel,
        name="local",
        out_shape=[jax.ShapeDtypeStruct((channels, edges), F32)] * 2,
        compiler_params=params,
        cost_estimate=pl.CostEstimate(flops=2**28, bytes_accessed=2**21, transcendentals=2**18),
    )(edge_vector, w_radial.T)
    node_out, edge_out, force = pl.pallas_call(
        functools.partial(main_kernel, peers, ecap, math.sqrt(NODE_DEV / EDGE_DEV)),
        name="main",
        out_shape=[
            jax.ShapeDtypeStruct((channels, nodes), BF),
            jax.ShapeDtypeStruct((channels, edges), BF),
            jax.ShapeDtypeStruct((peers, TERM, nodes), F32),
        ],
        scratch_shapes=[
            pltpu.VMEM((channels, edges), BF),
            pltpu.VMEM((channels, edges), F32),
            pltpu.VMEM((channels, peers * ecap), F32),
            pltpu.VMEM((groups * channels, low_in), BF),
            pltpu.VMEM((channels, trips), F32),
            pltpu.VMEM((low_out, groups * channels), F32),
            pltpu.VMEM((groups * channels, low_out), BF),
            pltpu.VMEM((1, edges), F32),
            pltpu.VMEM((low_in, groups * channels), F32),
            pltpu.VMEM((peers * TERM, nodes), F32),
        ],
        compiler_params=params,
    )(
        part,
        misc,
        radial,
        rate,
        edge_vector,
        own_node,
        own_edge,
        triplet_basis,
        w_radial.T,
        w_angle,
        w_energy.reshape(1, channels),
        triplet_in.reshape(1, trips),
        triplet_out.reshape(1, trips),
        target,
        *received,
    )
    force = add_over(force, "chan")
    mine = force[0]
    for d in range(1, peers):
        mine = mine + exchange(force[d], "graph", d)
    return node_out, edge_out, mine[0:3] + mine[3:6]


def solution(mesh):
    placed = (
        P(None, ("groups", "graph")),
        P(None, ("groups", "graph")),
        P(None, ("groups", "graph")),
        P(None, ("groups", "graph")),
        P(None, "chan"),
        P(None, "chan"),
        P(None, "chan"),
        P(None, "chan"),
        P(None, "chan"),
        P("chan"),
        P("groups", None, None),
        P("groups", None, None),
        P(("groups", "graph")),
        P(("groups", "graph")),
        P(("groups", "graph")),
        P(("groups", "graph")),
    )
    return jax.shard_map(
        shards,
        mesh=mesh,
        in_specs=placed,
        out_specs=(
            P("chan", ("groups", "graph")),
            P("chan", ("groups", "graph")),
            P(None, ("groups", "graph")),
        ),
        check_vma=False,
    )
```

```python
import functools
import math

import jax
import jax.numpy as jnp
from jax import lax
from jax.experimental import pallas as pl
from jax.experimental.pallas import tpu as pltpu
from jax.sharding import PartitionSpec as P

NODE_DEV = 256
EDGE_DEV = 2048

radius_max = 8.0
MISC = 16
TERM = 8
BF = jnp.bfloat16
F32 = jnp.float32
VMEM_LIMIT = 24 * 1024 * 1024


def sigmoid(values):
    return 1.0 / (1.0 + jnp.exp(-values))


def dot_tn(weight, data):
    return lax.dot_general(weight, data, (((0,), (0,)), ((), ())), preferred_element_type=F32)


def dot_nn(left, right):
    return lax.dot_general(left, right, (((1,), (0,)), ((), ())), preferred_element_type=F32)


def dot_nt(left, right):
    return lax.dot_general(left, right, (((1,), (1,)), ((), ())), preferred_element_type=F32)


def one_hot(row, count):
    lines = lax.broadcasted_iota(jnp.int32, (count, row.shape[1]), 0)
    return jnp.where(lines == row, 1.0, 0.0).astype(BF)


def choose(stacked, group, groups):
    rows = stacked.shape[0] // groups
    out = jnp.where(group == 0, stacked[:rows], 0.0)
    for g in range(1, groups):
        out = jnp.where(group == g, stacked[g * rows : (g + 1) * rows], out)
    return out


def expand(values, group, groups):
    zero = jnp.zeros_like(values)
    return jnp.concatenate([jnp.where(group == g, values, zero) for g in range(groups)], axis=0)


def halves(values):
    high = values.astype(BF)
    return high, (values - high.astype(F32)).astype(BF)


def radial_terms(squared, weight):
    count = weight.shape[1]
    lengths = jnp.sqrt(1.0 + squared)
    spread = 4.0 * radius_max / (count - 1)
    lines = lax.broadcasted_iota(jnp.int32, (count, 1), 0).astype(F32)
    centers = lines * (radius_max / (count - 1))
    offset = (lengths - centers) * (1.0 / spread)
    values = jnp.exp(-offset * offset)
    slopes = values * (offset * (-2.0 / spread))
    return dot_nn(weight, values.astype(BF)), dot_nn(weight, slopes.astype(BF)), lengths


def fetch(sources, places, sems):
    copies = [pltpu.make_async_copy(a, b, sems.at[i]) for i, (a, b) in enumerate(zip(sources, places))]
    for copy in copies:
        copy.start()
    return copies


def squared_length(vector):
    return vector[0:1] * vector[0:1] + vector[1:2] * vector[1:2] + vector[2:3] * vector[2:3]


def prep_kernel(peers, *refs):
    sources = refs[:10]
    part_out, misc_out, target_hot, own_node_out, own_edge_out = refs[10:15]
    sends = refs[15 : 15 + peers]
    places = refs[15 + peers : -1]
    sems = refs[-1]
    edge_source, edge = sources[9], places[9]
    edges = edge.shape[1]
    high_count = 4
    low_count = edges // high_count
    pieces = [slice(h * low_count, (h + 1) * low_count) for h in range(high_count)]
    copies = fetch(
        list(sources[:9]) + [edge_source.at[:, cols] for cols in pieces],
        list(places[:9]) + [edge.at[:, cols] for cols in pieces],
        sems,
    )
    node, w_source, w_target, w_edge, vector, node_send, edge_send, target, source = places[:9]
    me = lax.axis_index("graph")
    channels = w_source.shape[0]
    first_chan = pl.multiple_of(lax.axis_index("chan") * channels, channels)
    cap = node_send.shape[2]
    for copy in copies[:9]:
        copy.wait()
    own_node_out[...] = node[pl.ds(first_chan, channels), :]
    atoms = node[...]
    proj_src = dot_nn(w_source[...], atoms).astype(BF)
    dst_high, dst_low = halves(dot_nn(w_target[...], atoms))
    dst_table = jnp.concatenate([dst_high, dst_low], axis=0)
    own_nodes = jnp.concatenate([node_send[q, pl.ds(me, 1), :] for q in range(peers)], axis=0)
    own_nodes = own_nodes.astype(F32).astype(BF)
    parts = []
    for h, cols in enumerate(pieces):
        dst = target[:, cols]
        src = source[:, cols]
        hot = one_hot(dst, atoms.shape[1])
        target_hot[:, cols] = hot
        rows = dot_nn(dst_table, hot)
        src_peer = src // cap
        by_peer = dot_nn(own_nodes, one_hot(src - src_peer * cap, cap))
        src_node = choose(by_peer, src_peer, peers)
        vec = vector[:, cols]
        first = vec.astype(BF).astype(F32)
        second = (vec - first).astype(BF).astype(F32)
        third = vec - first - second
        misc = jnp.concatenate(
            [
                first,
                second,
                third,
                dst.astype(F32),
                src_node,
                src_peer.astype(F32),
                jnp.zeros((MISC - 12, low_count), F32),
            ],
            axis=0,
        )
        misc_out[:, cols] = misc
        copies[9 + h].wait()
        part = rows[:channels] + rows[channels:] + dot_nn(w_edge[...], edge[:, cols])
        part_out[:, cols] = part
        own_edge_out[:, cols] = edge[pl.ds(first_chan, channels), cols]
        parts.append(jnp.concatenate([part.astype(BF), misc.astype(BF)], axis=0))
    table = jnp.concatenate(parts, axis=0)
    for d in range(peers):
        chosen = edge_send[me, pl.ds(jnp.bitwise_xor(me, d), 1), :]
        high = jnp.where(chosen < 0, -1, chosen // low_count)
        picked = choose(dot_nn(table, one_hot(chosen % low_count, low_count)), high, high_count)
        sends[d][:channels] = proj_src
        sends[d][channels:] = picked.astype(BF)


def local_kernel(ecap, misc, *refs):
    sources = refs[:7]
    radial, rate, unit, angular, place_in, place_out, source_hot, radial_weight, energy_column = refs[7:16]
    places = refs[16:23]
    sems = refs[23]
    copies = fetch(sources, places, sems)
    vector, w_radial, w_angle, w_energy, trip_in, trip_out, basis = places
    me = lax.axis_index("graph")
    edges = vector.shape[1]
    trips = basis.shape[1]
    channels = w_radial.shape[0]
    width = 512
    for start in range(0, edges, width):
        cols = slice(start, start + width)
        source_hot[:, cols] = one_hot(misc[10:11, cols].astype(jnp.int32), source_hot.shape[0])
    for copy in copies:
        copy.wait()
    radial_weight[...] = w_radial[...]
    lines = lax.broadcasted_iota(jnp.int32, (channels, channels), 0)
    diagonal = lines == lax.broadcasted_iota(jnp.int32, (channels, channels), 1)
    energy_column[...] = jnp.sum(jnp.where(diagonal, w_energy[...], 0.0), axis=1, keepdims=True)
    for start in range(0, edges, width):
        cols = slice(start, start + width)
        vec = vector[:, cols]
        rows, slopes, lengths = radial_terms(squared_length(vec), w_radial[...])
        radial[:, cols] = rows
        rate[:, cols] = slopes
        unit[:, cols] = vec / lengths
    for start in range(0, trips, width):
        cols = slice(start, start + width)
        angular[:, cols] = dot_tn(w_angle[...], basis[:, cols])
        place_in[:, cols] = jnp.bitwise_xor(trip_in[:, cols], me * ecap)
        place_out[:, cols] = trip_out[:, cols]


def main_kernel(
    peers,
    ecap,
    scale,
    part,
    misc,
    target_hot,
    node,
    edge,
    radial,
    rate,
    unit,
    angular,
    place_in,
    place_out,
    source_hot,
    w_radial,
    w_energy,
    *refs,
):
    received = refs[:peers]
    node_out, edge_out, force_out = refs[peers : peers + 3]
    message, own_rate, slot_rate, slot_table, gather_sum, grad_table, edge_grad, slot_sum, moves = refs[peers + 3 :]
    me = lax.axis_index("graph")
    channels, edges = part.shape
    nodes = node.shape[1]
    trips = angular.shape[1]
    groups = slot_table.shape[0] // channels
    low_in = slot_table.shape[1]
    low_out = edges // groups
    step = 512
    width = min(1024, trips)
    turn_width = min(4096, trips)

    src_table = jnp.concatenate([received[d][:channels] for d in range(peers)], axis=0)

    def src_rows(hot, src_peer):
        return choose(dot_nn(src_table, hot), jnp.bitwise_xor(src_peer, me), peers)

    for start in range(0, edges, step):
        cols = slice(start, start + step)
        preact = src_rows(source_hot[:, cols], misc[11:12, cols].astype(jnp.int32)) + part[:, cols]
        active = preact * sigmoid(preact)
        message[:, cols] = (active * radial[:, cols]).astype(BF)
        own_rate[:, cols] = active * rate[:, cols]
    slots = []
    for d in range(peers):
        cols = slice(d * ecap, (d + 1) * ecap)
        extra = received[d][channels:].astype(F32)
        rest = extra[channels:]
        vec = rest[0:3] + rest[3:6] + rest[6:9]
        src_node = rest[10:11].astype(jnp.int32)
        src_peer = rest[11:12].astype(jnp.int32)
        slot_radial, slot_slope, lengths = radial_terms(squared_length(vec), w_radial[...])
        preact = src_rows(one_hot(src_node, nodes), src_peer) + extra[:channels]
        active = preact * sigmoid(preact)
        place = d * ecap
        low = place % low_in
        slot_table[(place // low_in) * channels : (place // low_in + 1) * channels, low : low + ecap] = (
            active * slot_radial
        ).astype(BF)
        slot_rate[:, cols] = active * slot_slope
        slots.append((vec / lengths, src_node, src_peer, rest[9:10].astype(jnp.int32)))

    def split(place, low_count):
        high = place // low_count
        return high, one_hot(place - high * low_count, low_count)

    gather_sum[...] = jnp.zeros_like(gather_sum)

    def forward(turn, carry):
        total = None
        for sub in range(turn_width // width):
            cols = pl.ds(pl.multiple_of(turn * turn_width + sub * width, width), width)
            high_in, hot_in = split(place_in[:, cols], low_in)
            high_out, hot_out = split(place_out[:, cols], low_out)
            rows = choose(dot_nn(slot_table[...], hot_in), high_in, groups)
            more = dot_nt(hot_out, expand((rows * angular[:, cols]).astype(BF), high_out, groups))
            total = more if total is None else total + more
        gather_sum[...] += total
        return carry

    lax.fori_loop(0, trips // turn_width, forward, 0)

    gathered = gather_sum[...].T
    atom_sum = jnp.zeros((channels, nodes), F32)
    for g in range(groups):
        cols = slice(g * low_out, (g + 1) * low_out)
        value = gathered[g * channels : (g + 1) * channels]
        fresh = edge[:, cols].astype(F32) + message[:, cols].astype(F32) + value * sigmoid(value)
        edge_out[:, cols] = fresh.astype(BF)
        high, low = halves(fresh)
        sums = dot_nt(jnp.concatenate([high, low], axis=0), target_hot[:, cols])
        atom_sum += sums[:channels] + sums[channels:]
    node_new = node[...].astype(F32) + scale * atom_sum
    node_out[...] = node_new.astype(BF)
    sig = sigmoid(node_new)
    grad_node = w_energy[...] * (sig * (1.0 + node_new * (1.0 - sig))) * scale
    high, low = halves(grad_node)
    grad_pair = jnp.concatenate([high, low], axis=0)
    for g in range(groups):
        cols = slice(g * low_out, (g + 1) * low_out)
        value = gathered[g * channels : (g + 1) * channels]
        rows = dot_nn(grad_pair, target_hot[:, cols])
        grad_edge = rows[:channels] + rows[channels:]
        sig = sigmoid(value)
        grad_table[g * channels : (g + 1) * channels, :] = (
            grad_edge * (sig * (1.0 + value * (1.0 - sig)))
        ).astype(BF)
        edge_grad[:, cols] = jnp.sum(grad_edge * own_rate[:, cols], axis=0, keepdims=True)

    slot_sum[...] = jnp.zeros_like(slot_sum)

    def backward(turn, carry):
        total = None
        for sub in range(turn_width // width):
            cols = pl.ds(pl.multiple_of(turn * turn_width + sub * width, width), width)
            high_in, hot_in = split(place_in[:, cols], low_in)
            high_out, hot_out = split(place_out[:, cols], low_out)
            rows = choose(dot_nn(grad_table[...], hot_out), high_out, groups)
            more = dot_nt(hot_in, expand((rows * angular[:, cols]).astype(BF), high_in, groups))
            total = more if total is None else total + more
        slot_sum[...] += total
        return carry

    lax.fori_loop(0, trips // turn_width, backward, 0)

    moves[...] = jnp.zeros_like(moves)

    def push_terms(push):
        high = push.astype(BF).astype(F32)
        return jnp.concatenate([high, push - high, jnp.zeros((TERM - 6, push.shape[1]), F32)], axis=0)

    for start in range(0, edges, step):
        cols = slice(start, start + step)
        terms = push_terms(unit[:, cols] * edge_grad[:, cols])
        src_peer = jnp.bitwise_xor(misc[11:12, cols].astype(jnp.int32), me)
        moves[...] += dot_nt(expand(terms, src_peer, peers).astype(BF), source_hot[:, cols])
        moves[:TERM] -= dot_nt(
            jnp.concatenate([terms, jnp.zeros_like(terms)], axis=0).astype(BF), target_hot[:, cols]
        )[:TERM]
    slot_grad = slot_sum[...].T
    for d in range(peers):
        cols = slice(d * ecap, (d + 1) * ecap)
        place = d * ecap
        low = place % low_in
        grads = slot_grad[(place // low_in) * channels : (place // low_in + 1) * channels, low : low + ecap]
        slot_unit, src_node, src_peer, dst_node = slots[d]
        terms = push_terms(slot_unit * jnp.sum(grads * slot_rate[:, cols], axis=0, keepdims=True))
        moves[...] += dot_nt(
            expand(terms, jnp.bitwise_xor(src_peer, me), peers).astype(BF), one_hot(src_node, nodes)
        )
        moves[d * TERM : (d + 1) * TERM] -= dot_nt(
            jnp.concatenate([terms, jnp.zeros_like(terms)], axis=0).astype(BF), one_hot(dst_node, nodes)
        )[:TERM]
    force_out[...] = moves[...].reshape(force_out.shape)


def exchange(values, axis, distance):
    count = lax.axis_size(axis)
    return lax.ppermute(values, axis, [(i, i ^ distance) for i in range(count)])


def add_over(values, axis):
    count = lax.axis_size(axis)
    if count <= 4:
        others = [exchange(values, axis, d) for d in range(1, count)]
        return functools.reduce(jnp.add, others, values)
    for bit in range(count.bit_length() - 1):
        values = values + exchange(values, axis, 1 << bit)
    return values


def shards(
    node_embed,
    edge_embed,
    edge_vector,
    triplet_basis,
    w_source,
    w_target,
    w_edge,
    w_radial,
    w_angle,
    w_energy,
    node_send,
    edge_send,
    edge_target,
    edge_source,
    triplet_in,
    triplet_out,
):
    peers = lax.axis_size("graph")
    channels = w_source.shape[1]
    nodes = node_embed.shape[1]
    edges = edge_embed.shape[1]
    trips = triplet_basis.shape[1]
    ecap = edge_send.shape[2]
    groups = 256 // channels
    low_in = peers * ecap // groups
    low_out = edges // groups
    shape = pltpu.VMEM
    params = pltpu.CompilerParams(vmem_limit_bytes=VMEM_LIMIT)

    def far(count):
        return [pl.BlockSpec(memory_space=pltpu.HBM)] * count

    def near(count):
        return [pl.BlockSpec(memory_space=pltpu.VMEM)] * count

    def buffers(arrays):
        return [pltpu.VMEM(a.shape, a.dtype) for a in arrays]

    inputs = [
        node_embed,
        w_source.T,
        w_target.T,
        w_edge.T,
        edge_vector,
        node_send,
        edge_send,
        edge_target.reshape(1, edges),
        edge_source.reshape(1, edges),
        edge_embed,
    ]
    part, misc, target_hot, own_node, own_edge, *sends = pl.pallas_call(
        functools.partial(prep_kernel, peers),
        name="prep",
        in_specs=far(len(inputs)),
        out_specs=near(5 + peers),
        out_shape=[
            shape((channels, edges), F32),
            shape((MISC, edges), F32),
            shape((nodes, edges), BF),
            shape((channels, nodes), BF),
            shape((channels, edges), BF),
        ]
        + [shape((2 * channels + MISC, ecap), BF)] * peers,
        scratch_shapes=buffers(inputs) + [pltpu.SemaphoreType.DMA((13,))],
        compiler_params=params,
    )(*[pltpu.with_memory_space_constraint(a, pltpu.HBM) for a in inputs])
    received = [sends[0]] + [exchange(sends[d], "graph", d) for d in range(1, peers)]
    inputs = [
        edge_vector,
        w_radial.T,
        w_angle,
        w_energy.reshape(1, channels),
        triplet_in.reshape(1, trips),
        triplet_out.reshape(1, trips),
        triplet_basis,
    ]
    local = pl.pallas_call(
        functools.partial(local_kernel, ecap),
        name="local",
        in_specs=near(1) + far(len(inputs)),
        out_specs=near(9),
        out_shape=[
            shape((channels, edges), F32),
            shape((channels, edges), F32),
            shape((3, edges), F32),
            shape((channels, trips), F32),
            shape((1, trips), jnp.int32),
            shape((1, trips), jnp.int32),
            shape((nodes, edges), BF),
            shape((channels, w_radial.shape[0]), BF),
            shape((channels, 1), F32),
        ],
        scratch_shapes=buffers(inputs) + [pltpu.SemaphoreType.DMA((7,))],
        compiler_params=params,
        cost_estimate=pl.CostEstimate(flops=2**30, bytes_accessed=2**23, transcendentals=2**18),
    )(misc, *[pltpu.with_memory_space_constraint(a, pltpu.HBM) for a in inputs])
    node_out, edge_out, force = pl.pallas_call(
        functools.partial(main_kernel, peers, ecap, math.sqrt(NODE_DEV / EDGE_DEV)),
        name="main",
        out_shape=[
            jax.ShapeDtypeStruct((channels, nodes), BF),
            jax.ShapeDtypeStruct((channels, edges), BF),
            shape((peers, TERM, nodes), F32),
        ],
        scratch_shapes=[
            pltpu.VMEM((channels, edges), BF),
            pltpu.VMEM((channels, edges), F32),
            pltpu.VMEM((channels, peers * ecap), F32),
            pltpu.VMEM((groups * channels, low_in), BF),
            pltpu.VMEM((low_out, groups * channels), F32),
            pltpu.VMEM((groups * channels, low_out), BF),
            pltpu.VMEM((1, edges), F32),
            pltpu.VMEM((low_in, groups * channels), F32),
            pltpu.VMEM((peers * TERM, nodes), F32),
        ],
        compiler_params=params,
    )(part, misc, target_hot, own_node, own_edge, *local, *received)
    force = add_over(force, "chan")
    mine = force[0]
    for d in range(1, peers):
        mine = mine + exchange(force[d], "graph", d)
    return node_out, edge_out, mine[0:3] + mine[3:6]


def solution(mesh):
    placed = (
        P(None, ("groups", "graph")),
        P(None, ("groups", "graph")),
        P(None, ("groups", "graph")),
        P(None, ("groups", "graph")),
        P(None, "chan"),
        P(None, "chan"),
        P(None, "chan"),
        P(None, "chan"),
        P(None, "chan"),
        P("chan"),
        P("groups", None, None),
        P("groups", None, None),
        P(("groups", "graph")),
        P(("groups", "graph")),
        P(("groups", "graph")),
        P(("groups", "graph")),
    )
    return jax.shard_map(
        shards,
        mesh=mesh,
        in_specs=placed,
        out_specs=(
            P("chan", ("groups", "graph")),
            P("chan", ("groups", "graph")),
            P(None, ("groups", "graph")),
        ),
        check_vma=False,
    )
```

```python
import functools
import math

import jax
import jax.numpy as jnp
from jax import lax
from jax.experimental import pallas as pl
from jax.experimental.pallas import tpu as pltpu
from jax.sharding import PartitionSpec as P

NODE_DEV = 256
EDGE_DEV = 2048

radius_max = 8.0
MISC = 16
TERM = 8
BF = jnp.bfloat16
F32 = jnp.float32
VMEM_LIMIT = 24 * 1024 * 1024
GIN_F, GOUT_F, GOUT_B, GIN_B = 1, 2, 1, 1
WF = 2048
WB = 2048
TURN_F = 8192
TURN_B = 8192


def sigmoid(values):
    return 1.0 / (1.0 + jnp.exp(-values))


def dot_tn(weight, data):
    return lax.dot_general(weight, data, (((0,), (0,)), ((), ())), preferred_element_type=F32)


def dot_nn(left, right):
    return lax.dot_general(left, right, (((1,), (0,)), ((), ())), preferred_element_type=F32)


def dot_nt(left, right):
    return lax.dot_general(left, right, (((1,), (1,)), ((), ())), preferred_element_type=F32)


def one_hot(row, count):
    lines = lax.broadcasted_iota(jnp.int16, (count, row.shape[1]), 0)
    one = jnp.ones((count, row.shape[1]), BF)
    return jnp.where(lines == row.astype(jnp.int16), one, jnp.zeros_like(one))


def choose(stacked, group, groups):
    rows = stacked.shape[0] // groups
    out = jnp.where(group == 0, stacked[:rows], 0.0)
    for g in range(1, groups):
        out = jnp.where(group == g, stacked[g * rows : (g + 1) * rows], out)
    return out


def expand(values, group, groups):
    zero = jnp.zeros_like(values)
    return jnp.concatenate([jnp.where(group == g, values, zero) for g in range(groups)], axis=0)


def halves(values):
    high = values.astype(BF)
    return high, (values - high.astype(F32)).astype(BF)


def radial_terms(squared, weight):
    count = weight.shape[1]
    lengths = jnp.sqrt(1.0 + squared)
    spread = 4.0 * radius_max / (count - 1)
    lines = lax.broadcasted_iota(jnp.int32, (count, 1), 0).astype(F32)
    centers = lines * (radius_max / (count - 1))
    offset = (lengths - centers) * (1.0 / spread)
    values = jnp.exp(-offset * offset)
    slopes = values * (offset * (-2.0 / spread))
    return dot_nn(weight, values.astype(BF)), dot_nn(weight, slopes.astype(BF)), lengths


def fetch(sources, places, sems):
    copies = [pltpu.make_async_copy(a, b, sems.at[i]) for i, (a, b) in enumerate(zip(sources, places))]
    for copy in copies:
        copy.start()
    return copies


def squared_length(vector):
    return vector[0:1] * vector[0:1] + vector[1:2] * vector[1:2] + vector[2:3] * vector[2:3]


def prep_kernel(peers, *refs):
    sources = refs[:10]
    part_out, misc_out, target_hot, own_node_out, own_edge_out = refs[10:15]
    sends = refs[15 : 15 + peers]
    places = refs[15 + peers : -1]
    sems = refs[-1]
    edge_source, edge = sources[9], places[9]
    edges = edge.shape[1]
    high_count = 4
    low_count = edges // high_count
    pieces = [slice(h * low_count, (h + 1) * low_count) for h in range(high_count)]
    copies = fetch(
        list(sources[:9]) + [edge_source.at[:, cols] for cols in pieces],
        list(places[:9]) + [edge.at[:, cols] for cols in pieces],
        sems,
    )
    node, w_source, w_target, w_edge, vector, node_send, edge_send, target, source = places[:9]
    me = lax.axis_index("graph")
    channels = w_source.shape[0]
    first_chan = pl.multiple_of(lax.axis_index("chan") * channels, channels)
    cap = node_send.shape[2]
    for copy in copies[:9]:
        copy.wait()
    own_node_out[...] = node[pl.ds(first_chan, channels), :]
    atoms = node[...]
    proj_src = dot_nn(w_source[...], atoms).astype(BF)
    dst_high, dst_low = halves(dot_nn(w_target[...], atoms))
    dst_table = jnp.concatenate([dst_high, dst_low], axis=0)
    own_nodes = jnp.concatenate([node_send[q, pl.ds(me, 1), :] for q in range(peers)], axis=0)
    own_nodes = own_nodes.astype(F32).astype(BF)
    parts = []
    for h, cols in enumerate(pieces):
        dst = target[:, cols]
        src = source[:, cols]
        hot = one_hot(dst, atoms.shape[1])
        target_hot[:, cols] = hot
        rows = dot_nn(dst_table, hot)
        src_peer = src // cap
        by_peer = dot_nn(own_nodes, one_hot(src - src_peer * cap, cap))
        src_node = choose(by_peer, src_peer, peers)
        vec = vector[:, cols]
        first = vec.astype(BF).astype(F32)
        second = (vec - first).astype(BF).astype(F32)
        third = vec - first - second
        misc = jnp.concatenate(
            [
                first,
                second,
                third,
                dst.astype(F32),
                src_node,
                src_peer.astype(F32),
                jnp.zeros((MISC - 12, low_count), F32),
            ],
            axis=0,
        )
        misc_out[:, cols] = misc
        copies[9 + h].wait()
        part = rows[:channels] + rows[channels:] + dot_nn(w_edge[...], edge[:, cols])
        part_out[:, cols] = part
        own_edge_out[:, cols] = edge[pl.ds(first_chan, channels), cols]
        parts.append(jnp.concatenate([part.astype(BF), misc.astype(BF)], axis=0))
    table = jnp.concatenate(parts, axis=0)
    for d in range(peers):
        chosen = edge_send[me, pl.ds(jnp.bitwise_xor(me, d), 1), :]
        high = jnp.where(chosen < 0, -1, chosen // low_count)
        picked = choose(dot_nn(table, one_hot(chosen % low_count, low_count)), high, high_count)
        sends[d][:channels] = proj_src
        sends[d][channels:] = picked.astype(BF)


def local_kernel(ecap, misc, *refs):
    sources = refs[:7]
    radial, rate, unit, angular, place_in, place_out, source_hot, radial_weight, energy_column = refs[7:16]
    places = refs[16:23]
    sems = refs[23]
    copies = fetch(sources, places, sems)
    vector, w_radial, w_angle, w_energy, trip_in, trip_out, basis = places
    me = lax.axis_index("graph")
    edges = vector.shape[1]
    trips = basis.shape[1]
    channels = w_radial.shape[0]
    width = 512
    for start in range(0, edges, width):
        cols = slice(start, start + width)
        source_hot[:, cols] = one_hot(misc[10:11, cols].astype(jnp.int32), source_hot.shape[0])
    for copy in copies:
        copy.wait()
    radial_weight[...] = w_radial[...]
    lines = lax.broadcasted_iota(jnp.int32, (channels, channels), 0)
    diagonal = lines == lax.broadcasted_iota(jnp.int32, (channels, channels), 1)
    energy_column[...] = jnp.sum(jnp.where(diagonal, w_energy[...], 0.0), axis=1, keepdims=True)
    for start in range(0, edges, width):
        cols = slice(start, start + width)
        vec = vector[:, cols]
        rows, slopes, lengths = radial_terms(squared_length(vec), w_radial[...])
        radial[:, cols] = rows
        rate[:, cols] = slopes
        unit[:, cols] = vec / lengths
    for start in range(0, trips, width):
        cols = slice(start, start + width)
        angular[:, cols] = dot_tn(w_angle[...], basis[:, cols])
        place_in[:, cols] = jnp.bitwise_xor(trip_in[:, cols], me * ecap)
        place_out[:, cols] = trip_out[:, cols]


def keep(table, start, values):
    channels, count = values.shape
    low = table.shape[1]
    piece = min(low, count)
    for at in range(0, count, piece):
        group, off = divmod(start + at, low)
        table[group * channels : (group + 1) * channels, off : off + piece] = values[:, at : at + piece]


def part_of(table, channels, start, count):
    low = table.shape[1]
    piece = min(low, count)
    out = []
    for at in range(start, start + count, piece):
        group, off = divmod(at, low)
        out.append(table[group * channels : (group + 1) * channels, off : off + piece])
    return jnp.concatenate(out, axis=1) if len(out) > 1 else out[0]


def main_kernel(
    peers,
    ecap,
    scale,
    part,
    misc,
    target_hot,
    node,
    edge,
    radial,
    rate,
    unit,
    angular,
    place_in,
    place_out,
    source_hot,
    w_radial,
    w_energy,
    *refs,
):
    received = refs[:peers]
    node_out, edge_out, force_out = refs[peers : peers + 3]
    message, own_rate, slot_rate, slot_table, gather_sum, grad_table, edge_grad, slot_sum, moves = refs[peers + 3 :]
    me = lax.axis_index("graph")
    channels, edges = part.shape
    nodes = node.shape[1]
    trips = angular.shape[1]
    get_in, low_in = slot_table.shape[0] // channels, slot_table.shape[1]
    put_out, low_put = gather_sum.shape[1] // channels, gather_sum.shape[0]
    get_out, low_get = grad_table.shape[0] // channels, grad_table.shape[1]
    put_in, low_back = slot_sum.shape[1] // channels, slot_sum.shape[0]
    step = 512

    src_table = jnp.concatenate([received[d][:channels] for d in range(peers)], axis=0)

    def src_rows(hot, src_peer):
        return choose(dot_nn(src_table, hot), jnp.bitwise_xor(src_peer, me), peers)

    for start in range(0, edges, step):
        cols = slice(start, start + step)
        preact = src_rows(source_hot[:, cols], misc[11:12, cols].astype(jnp.int32)) + part[:, cols]
        active = preact * sigmoid(preact)
        message[:, cols] = (active * radial[:, cols]).astype(BF)
        own_rate[:, cols] = active * rate[:, cols]
    slots = []
    for d in range(peers):
        cols = slice(d * ecap, (d + 1) * ecap)
        extra = received[d][channels:].astype(F32)
        rest = extra[channels:]
        vec = rest[0:3] + rest[3:6] + rest[6:9]
        src_node = rest[10:11].astype(jnp.int32)
        src_peer = rest[11:12].astype(jnp.int32)
        slot_radial, slot_slope, lengths = radial_terms(squared_length(vec), w_radial[...])
        preact = src_rows(one_hot(src_node, nodes), src_peer) + extra[:channels]
        active = preact * sigmoid(preact)
        keep(slot_table, d * ecap, (active * slot_radial).astype(BF))
        slot_rate[:, cols] = active * slot_slope
        slots.append((vec / lengths, src_node, src_peer, rest[9:10].astype(jnp.int32)))

    def split(place, low_count):
        high = place // low_count
        return high, one_hot(place - high * low_count, low_count)

    def sweep(total, table, get_place, get_groups, put_place, put_groups, width, turn_width):
        width, turn_width = min(width, trips), min(turn_width, trips)
        total[...] = jnp.zeros_like(total)

        def turn(number, carry):
            found = None
            for sub in range(turn_width // width):
                cols = pl.ds(pl.multiple_of(number * turn_width + sub * width, width), width)
                high_get, hot_get = split(get_place[:, cols], table.shape[1])
                high_put, hot_put = split(put_place[:, cols], total.shape[0])
                term = choose(dot_nn(table[...], hot_get), high_get, get_groups) * angular[:, cols]
                more = dot_nt(hot_put, expand(term.astype(BF), high_put, put_groups))
                found = more if found is None else found + more
            total[...] += found
            return carry

        lax.fori_loop(0, trips // turn_width, turn, 0)

    sweep(gather_sum, slot_table, place_in, get_in, place_out, put_out, WF, TURN_F)

    gathered = gather_sum[...].T
    atom_sum = jnp.zeros((channels, nodes), F32)
    for start in range(0, edges, step):
        cols = slice(start, start + step)
        value = part_of(gathered, channels, start, step)
        fresh = edge[:, cols].astype(F32) + message[:, cols].astype(F32) + value * sigmoid(value)
        edge_out[:, cols] = fresh.astype(BF)
        high, low = halves(fresh)
        sums = dot_nt(jnp.concatenate([high, low], axis=0), target_hot[:, cols])
        atom_sum += sums[:channels] + sums[channels:]
    node_new = node[...].astype(F32) + scale * atom_sum
    node_out[...] = node_new.astype(BF)
    sig = sigmoid(node_new)
    grad_node = w_energy[...] * (sig * (1.0 + node_new * (1.0 - sig))) * scale
    high, low = halves(grad_node)
    grad_pair = jnp.concatenate([high, low], axis=0)
    for start in range(0, edges, step):
        cols = slice(start, start + step)
        value = part_of(gathered, channels, start, step)
        rows = dot_nn(grad_pair, target_hot[:, cols])
        grad_edge = rows[:channels] + rows[channels:]
        sig = sigmoid(value)
        keep(grad_table, start, (grad_edge * (sig * (1.0 + value * (1.0 - sig)))).astype(BF))
        edge_grad[:, cols] = jnp.sum(grad_edge * own_rate[:, cols], axis=0, keepdims=True)

    sweep(slot_sum, grad_table, place_out, get_out, place_in, put_in, WB, TURN_B)

    moves[...] = jnp.zeros_like(moves)

    def push_terms(push):
        high = push.astype(BF).astype(F32)
        return jnp.concatenate([high, push - high, jnp.zeros((TERM - 6, push.shape[1]), F32)], axis=0)

    for start in range(0, edges, step):
        cols = slice(start, start + step)
        terms = push_terms(unit[:, cols] * edge_grad[:, cols])
        src_peer = jnp.bitwise_xor(misc[11:12, cols].astype(jnp.int32), me)
        moves[...] += dot_nt(expand(terms, src_peer, peers).astype(BF), source_hot[:, cols])
        moves[:TERM] -= dot_nt(
            jnp.concatenate([terms, jnp.zeros_like(terms)], axis=0).astype(BF), target_hot[:, cols]
        )[:TERM]
    slot_grad = slot_sum[...].T
    for d in range(peers):
        cols = slice(d * ecap, (d + 1) * ecap)
        grads = part_of(slot_grad, channels, d * ecap, ecap)
        slot_unit, src_node, src_peer, dst_node = slots[d]
        terms = push_terms(slot_unit * jnp.sum(grads * slot_rate[:, cols], axis=0, keepdims=True))
        moves[...] += dot_nt(
            expand(terms, jnp.bitwise_xor(src_peer, me), peers).astype(BF), one_hot(src_node, nodes)
        )
        moves[d * TERM : (d + 1) * TERM] -= dot_nt(
            jnp.concatenate([terms, jnp.zeros_like(terms)], axis=0).astype(BF), one_hot(dst_node, nodes)
        )[:TERM]
    force_out[...] = moves[...].reshape(force_out.shape)


def exchange(values, axis, distance):
    count = lax.axis_size(axis)
    return lax.ppermute(values, axis, [(i, i ^ distance) for i in range(count)])


def add_over(values, axis):
    count = lax.axis_size(axis)
    if count <= 4:
        others = [exchange(values, axis, d) for d in range(1, count)]
        return functools.reduce(jnp.add, others, values)
    for bit in range(count.bit_length() - 1):
        values = values + exchange(values, axis, 1 << bit)
    return values


def shards(
    node_embed,
    edge_embed,
    edge_vector,
    triplet_basis,
    w_source,
    w_target,
    w_edge,
    w_radial,
    w_angle,
    w_energy,
    node_send,
    edge_send,
    edge_target,
    edge_source,
    triplet_in,
    triplet_out,
):
    peers = lax.axis_size("graph")
    channels = w_source.shape[1]
    nodes = node_embed.shape[1]
    edges = edge_embed.shape[1]
    trips = triplet_basis.shape[1]
    ecap = edge_send.shape[2]
    groups = 256 // channels
    slots = peers * ecap
    tables = [GIN_F * groups, GOUT_F * groups, GOUT_B * groups, GIN_B * groups]
    shape = pltpu.VMEM
    params = pltpu.CompilerParams(vmem_limit_bytes=VMEM_LIMIT)

    def far(count):
        return [pl.BlockSpec(memory_space=pltpu.HBM)] * count

    def near(count):
        return [pl.BlockSpec(memory_space=pltpu.VMEM)] * count

    def buffers(arrays):
        return [pltpu.VMEM(a.shape, a.dtype) for a in arrays]

    inputs = [
        node_embed,
        w_source.T,
        w_target.T,
        w_edge.T,
        edge_vector,
        node_send,
        edge_send,
        edge_target.reshape(1, edges),
        edge_source.reshape(1, edges),
        edge_embed,
    ]
    part, misc, target_hot, own_node, own_edge, *sends = pl.pallas_call(
        functools.partial(prep_kernel, peers),
        name="prep",
        in_specs=far(len(inputs)),
        out_specs=near(5 + peers),
        out_shape=[
            shape((channels, edges), F32),
            shape((MISC, edges), F32),
            shape((nodes, edges), BF),
            shape((channels, nodes), BF),
            shape((channels, edges), BF),
        ]
        + [shape((2 * channels + MISC, ecap), BF)] * peers,
        scratch_shapes=buffers(inputs) + [pltpu.SemaphoreType.DMA((13,))],
        compiler_params=params,
    )(*[pltpu.with_memory_space_constraint(a, pltpu.HBM) for a in inputs])
    received = [sends[0]] + [exchange(sends[d], "graph", d) for d in range(1, peers)]
    inputs = [
        edge_vector,
        w_radial.T,
        w_angle,
        w_energy.reshape(1, channels),
        triplet_in.reshape(1, trips),
        triplet_out.reshape(1, trips),
        triplet_basis,
    ]
    local = pl.pallas_call(
        functools.partial(local_kernel, ecap),
        name="local",
        in_specs=near(1) + far(len(inputs)),
        out_specs=near(9),
        out_shape=[
            shape((channels, edges), F32),
            shape((channels, edges), F32),
            shape((3, edges), F32),
            shape((channels, trips), F32),
            shape((1, trips), jnp.int32),
            shape((1, trips), jnp.int32),
            shape((nodes, edges), BF),
            shape((channels, w_radial.shape[0]), BF),
            shape((channels, 1), F32),
        ],
        scratch_shapes=buffers(inputs) + [pltpu.SemaphoreType.DMA((7,))],
        compiler_params=params,
        cost_estimate=pl.CostEstimate(flops=2**30, bytes_accessed=2**23, transcendentals=2**18),
    )(misc, *[pltpu.with_memory_space_constraint(a, pltpu.HBM) for a in inputs])
    node_out, edge_out, force = pl.pallas_call(
        functools.partial(main_kernel, peers, ecap, math.sqrt(NODE_DEV / EDGE_DEV)),
        name="main",
        out_shape=[
            jax.ShapeDtypeStruct((channels, nodes), BF),
            jax.ShapeDtypeStruct((channels, edges), BF),
            shape((peers, TERM, nodes), F32),
        ],
        scratch_shapes=[
            pltpu.VMEM((channels, edges), BF),
            pltpu.VMEM((channels, edges), F32),
            pltpu.VMEM((channels, slots), F32),
            pltpu.VMEM((tables[0] * channels, slots // tables[0]), BF),
            pltpu.VMEM((edges // tables[1], tables[1] * channels), F32),
            pltpu.VMEM((tables[2] * channels, edges // tables[2]), BF),
            pltpu.VMEM((1, edges), F32),
            pltpu.VMEM((slots // tables[3], tables[3] * channels), F32),
            pltpu.VMEM((peers * TERM, nodes), F32),
        ],
        compiler_params=params,
    )(part, misc, target_hot, own_node, own_edge, *local, *received)
    force = add_over(force, "chan")
    mine = force[0]
    for d in range(1, peers):
        mine = mine + exchange(force[d], "graph", d)
    return node_out, edge_out, mine[0:3] + mine[3:6]


def solution(mesh):
    placed = (
        P(None, ("groups", "graph")),
        P(None, ("groups", "graph")),
        P(None, ("groups", "graph")),
        P(None, ("groups", "graph")),
        P(None, "chan"),
        P(None, "chan"),
        P(None, "chan"),
        P(None, "chan"),
        P(None, "chan"),
        P("chan"),
        P("groups", None, None),
        P("groups", None, None),
        P(("groups", "graph")),
        P(("groups", "graph")),
        P(("groups", "graph")),
        P(("groups", "graph")),
    )
    return jax.shard_map(
        shards,
        mesh=mesh,
        in_specs=placed,
        out_specs=(
            P("chan", ("groups", "graph")),
            P("chan", ("groups", "graph")),
            P(None, ("groups", "graph")),
        ),
        check_vma=False,
    )
```

```python
import functools
import math

import jax
import jax.numpy as jnp
from jax import lax
from jax.experimental import pallas as pl
from jax.experimental.pallas import tpu as pltpu
from jax.sharding import PartitionSpec as P

NODE_DEV = 256
EDGE_DEV = 2048

radius_max = 8.0
MISC = 16
TERM = 8
BF = jnp.bfloat16
F32 = jnp.float32
VMEM_LIMIT = 24 * 1024 * 1024
GRAPH_ORDER, CHAN_ORDER = "213", "123"
GIN_F, GOUT_F, GOUT_B, GIN_B = 1, 2, 1, 1
WF = 2048
WB = 2048
TURN_F = 8192
TURN_B = 8192


def sigmoid(values):
    return 1.0 / (1.0 + jnp.exp(-values))


def dot_tn(weight, data):
    return lax.dot_general(weight, data, (((0,), (0,)), ((), ())), preferred_element_type=F32)


def dot_nn(left, right):
    return lax.dot_general(left, right, (((1,), (0,)), ((), ())), preferred_element_type=F32)


def dot_nt(left, right):
    return lax.dot_general(left, right, (((1,), (1,)), ((), ())), preferred_element_type=F32)


def one_hot(row, count):
    lines = lax.broadcasted_iota(jnp.int16, (count, row.shape[1]), 0)
    one = jnp.ones((count, row.shape[1]), BF)
    return jnp.where(lines == row.astype(jnp.int16), one, jnp.zeros_like(one))


def choose(stacked, group, groups):
    rows = stacked.shape[0] // groups
    out = jnp.where(group == 0, stacked[:rows], 0.0)
    for g in range(1, groups):
        out = jnp.where(group == g, stacked[g * rows : (g + 1) * rows], out)
    return out


def expand(values, group, groups):
    zero = jnp.zeros_like(values)
    return jnp.concatenate([jnp.where(group == g, values, zero) for g in range(groups)], axis=0)


def halves(values):
    high = values.astype(BF)
    return high, (values - high.astype(F32)).astype(BF)


def radial_terms(squared, weight):
    count = weight.shape[1]
    lengths = jnp.sqrt(1.0 + squared)
    spread = 4.0 * radius_max / (count - 1)
    lines = lax.broadcasted_iota(jnp.int32, (count, 1), 0).astype(F32)
    centers = lines * (radius_max / (count - 1))
    offset = (lengths - centers) * (1.0 / spread)
    values = jnp.exp(-offset * offset)
    slopes = values * (offset * (-2.0 / spread))
    return dot_nn(weight, values.astype(BF)), dot_nn(weight, slopes.astype(BF)), lengths


def fetch(sources, places, sems):
    copies = [pltpu.make_async_copy(a, b, sems.at[i]) for i, (a, b) in enumerate(zip(sources, places))]
    for copy in copies:
        copy.start()
    return copies


def squared_length(vector):
    return vector[0:1] * vector[0:1] + vector[1:2] * vector[1:2] + vector[2:3] * vector[2:3]


def prep_kernel(peers, *refs):
    sources = refs[:10]
    part_out, misc_out, target_hot, own_node_out, own_edge_out = refs[10:15]
    sends = refs[15 : 15 + peers]
    places = refs[15 + peers : -1]
    sems = refs[-1]
    edge_source, edge = sources[9], places[9]
    edges = edge.shape[1]
    high_count = 4
    low_count = edges // high_count
    pieces = [slice(h * low_count, (h + 1) * low_count) for h in range(high_count)]
    copies = fetch(
        list(sources[4:9]) + list(sources[:4]) + [edge_source.at[:, cols] for cols in pieces],
        list(places[4:9]) + list(places[:4]) + [edge.at[:, cols] for cols in pieces],
        sems,
    )
    copies = copies[5:9] + copies[:5] + copies[9:]
    node, w_source, w_target, w_edge, vector, node_send, edge_send, target, source = places[:9]
    me = lax.axis_index("graph")
    channels = w_source.shape[0]
    first_chan = pl.multiple_of(lax.axis_index("chan") * channels, channels)
    cap = node_send.shape[2]
    for copy in copies[4:9]:
        copy.wait()
    own_nodes = jnp.concatenate([node_send[q, pl.ds(me, 1), :] for q in range(peers)], axis=0)
    own_nodes = own_nodes.astype(F32).astype(BF)
    miscs = []
    for cols in pieces:
        dst = target[:, cols]
        src = source[:, cols]
        target_hot[:, cols] = one_hot(dst, target_hot.shape[0])
        src_peer = src // cap
        by_peer = dot_nn(own_nodes, one_hot(src - src_peer * cap, cap))
        src_node = choose(by_peer, src_peer, peers)
        vec = vector[:, cols]
        first = vec.astype(BF).astype(F32)
        second = (vec - first).astype(BF).astype(F32)
        third = vec - first - second
        misc = jnp.concatenate(
            [
                first,
                second,
                third,
                dst.astype(F32),
                src_node,
                src_peer.astype(F32),
                jnp.zeros((MISC - 12, low_count), F32),
            ],
            axis=0,
        )
        misc_out[:, cols] = misc
        miscs.append(misc.astype(BF))
    picks = []
    for d in range(peers):
        chosen = edge_send[me, pl.ds(jnp.bitwise_xor(me, d), 1), :]
        high = jnp.where(chosen < 0, -1, chosen // low_count)
        picks.append((high, one_hot(chosen % low_count, low_count)))
    for copy in copies[:4]:
        copy.wait()
    own_node_out[...] = node[pl.ds(first_chan, channels), :]
    atoms = node[...]
    proj_src = dot_nn(w_source[...], atoms).astype(BF)
    dst_high, dst_low = halves(dot_nn(w_target[...], atoms))
    dst_table = jnp.concatenate([dst_high, dst_low], axis=0)
    for d in range(peers):
        sends[d][:channels] = proj_src
    parts = []
    for h, cols in enumerate(pieces):
        rows = dot_nn(dst_table, target_hot[:, cols])
        copies[9 + h].wait()
        part = rows[:channels] + rows[channels:] + dot_nn(w_edge[...], edge[:, cols])
        part_out[:, cols] = part
        own_edge_out[:, cols] = edge[pl.ds(first_chan, channels), cols]
        parts.append(jnp.concatenate([part.astype(BF), miscs[h]], axis=0))
    table = jnp.concatenate(parts, axis=0)
    for d, (high, hot) in enumerate(picks):
        sends[d][channels:] = choose(dot_nn(table, hot), high, high_count).astype(BF)


def local_kernel(ecap, misc, *refs):
    sources = refs[:7]
    radial, rate, unit, angular, place_in, place_out, source_hot, radial_weight, energy_column = refs[7:16]
    places = refs[16:23]
    sems = refs[23]
    copies = fetch(sources, places, sems)
    vector, w_radial, w_angle, w_energy, trip_in, trip_out, basis = places
    me = lax.axis_index("graph")
    edges = vector.shape[1]
    trips = basis.shape[1]
    channels = w_radial.shape[0]
    width = 512
    for start in range(0, edges, width):
        cols = slice(start, start + width)
        source_hot[:, cols] = one_hot(misc[10:11, cols].astype(jnp.int32), source_hot.shape[0])
    for copy in copies:
        copy.wait()
    radial_weight[...] = w_radial[...]
    lines = lax.broadcasted_iota(jnp.int32, (channels, channels), 0)
    diagonal = lines == lax.broadcasted_iota(jnp.int32, (channels, channels), 1)
    energy_column[...] = jnp.sum(jnp.where(diagonal, w_energy[...], 0.0), axis=1, keepdims=True)
    for start in range(0, edges, width):
        cols = slice(start, start + width)
        vec = vector[:, cols]
        rows, slopes, lengths = radial_terms(squared_length(vec), w_radial[...])
        radial[:, cols] = rows
        rate[:, cols] = slopes
        unit[:, cols] = vec / lengths
    for start in range(0, trips, width):
        cols = slice(start, start + width)
        angular[:, cols] = dot_tn(w_angle[...], basis[:, cols])
        place_in[:, cols] = jnp.bitwise_xor(trip_in[:, cols], me * ecap)
        place_out[:, cols] = trip_out[:, cols]


def keep(table, start, values):
    channels, count = values.shape
    low = table.shape[1]
    piece = min(low, count)
    for at in range(0, count, piece):
        group, off = divmod(start + at, low)
        table[group * channels : (group + 1) * channels, off : off + piece] = values[:, at : at + piece]


def part_of(table, channels, start, count):
    low = table.shape[1]
    piece = min(low, count)
    out = []
    for at in range(start, start + count, piece):
        group, off = divmod(at, low)
        out.append(table[group * channels : (group + 1) * channels, off : off + piece])
    return jnp.concatenate(out, axis=1) if len(out) > 1 else out[0]


def main_kernel(
    peers,
    ecap,
    scale,
    part,
    misc,
    target_hot,
    node,
    edge,
    radial,
    rate,
    unit,
    angular,
    place_in,
    place_out,
    source_hot,
    w_radial,
    w_energy,
    *refs,
):
    received = refs[:peers]
    node_out, edge_out, force_out = refs[peers : peers + 3]
    message, own_rate, slot_rate, slot_table, gather_sum, grad_table, edge_grad, slot_sum, moves = refs[peers + 3 :]
    me = lax.axis_index("graph")
    channels, edges = part.shape
    nodes = node.shape[1]
    trips = angular.shape[1]
    get_in, low_in = slot_table.shape[0] // channels, slot_table.shape[1]
    put_out, low_put = gather_sum.shape[1] // channels, gather_sum.shape[0]
    get_out, low_get = grad_table.shape[0] // channels, grad_table.shape[1]
    put_in, low_back = slot_sum.shape[1] // channels, slot_sum.shape[0]
    step = 256

    src_table = jnp.concatenate([received[d][:channels] for d in range(peers)], axis=0)

    def src_rows(hot, src_peer):
        return choose(dot_nn(src_table, hot), jnp.bitwise_xor(src_peer, me), peers)

    for start in range(0, edges, step):
        cols = slice(start, start + step)
        preact = src_rows(source_hot[:, cols], misc[11:12, cols].astype(jnp.int32)) + part[:, cols]
        active = preact * sigmoid(preact)
        message[:, cols] = (active * radial[:, cols]).astype(BF)
        own_rate[:, cols] = active * rate[:, cols]
    slots = []
    for d in range(peers):
        cols = slice(d * ecap, (d + 1) * ecap)
        extra = received[d][channels:].astype(F32)
        rest = extra[channels:]
        vec = rest[0:3] + rest[3:6] + rest[6:9]
        src_node = rest[10:11].astype(jnp.int32)
        src_peer = rest[11:12].astype(jnp.int32)
        slot_radial, slot_slope, lengths = radial_terms(squared_length(vec), w_radial[...])
        preact = src_rows(one_hot(src_node, nodes), src_peer) + extra[:channels]
        active = preact * sigmoid(preact)
        keep(slot_table, d * ecap, (active * slot_radial).astype(BF))
        slot_rate[:, cols] = active * slot_slope
        slots.append((vec / lengths, src_node, src_peer, rest[9:10].astype(jnp.int32)))

    def split(place, low_count):
        high = place // low_count
        return high, one_hot(place - high * low_count, low_count)

    def sweep(total, table, get_place, get_groups, put_place, put_groups, width, turn_width):
        width, turn_width = min(width, trips), min(turn_width, trips)

        def turn(number):
            found = None
            for sub in range(turn_width // width):
                cols = slice(number * turn_width + sub * width, number * turn_width + (sub + 1) * width)
                high_get, hot_get = split(get_place[:, cols], table.shape[1])
                high_put, hot_put = split(put_place[:, cols], total.shape[0])
                term = choose(dot_nn(table[...], hot_get), high_get, get_groups) * angular[:, cols]
                more = dot_nt(hot_put, expand(term.astype(BF), high_put, put_groups))
                found = more if found is None else found + more
            return found

        total[...] = functools.reduce(jnp.add, [turn(number) for number in range(trips // turn_width)])

    sweep(gather_sum, slot_table, place_in, get_in, place_out, put_out, WF, TURN_F)

    gathered = gather_sum[...].T
    atom_sum = jnp.zeros((channels, nodes), F32)
    for start in range(0, edges, step):
        cols = slice(start, start + step)
        value = part_of(gathered, channels, start, step)
        fresh = edge[:, cols].astype(F32) + message[:, cols].astype(F32) + value * sigmoid(value)
        edge_out[:, cols] = fresh.astype(BF)
        high, low = halves(fresh)
        sums = dot_nt(jnp.concatenate([high, low], axis=0), target_hot[:, cols])
        atom_sum += sums[:channels] + sums[channels:]
    node_new = node[...].astype(F32) + scale * atom_sum
    node_out[...] = node_new.astype(BF)
    sig = sigmoid(node_new)
    grad_node = w_energy[...] * (sig * (1.0 + node_new * (1.0 - sig))) * scale
    high, low = halves(grad_node)
    grad_pair = jnp.concatenate([high, low], axis=0)
    for start in range(0, edges, step):
        cols = slice(start, start + step)
        value = part_of(gathered, channels, start, step)
        rows = dot_nn(grad_pair, target_hot[:, cols])
        grad_edge = rows[:channels] + rows[channels:]
        sig = sigmoid(value)
        keep(grad_table, start, (grad_edge * (sig * (1.0 + value * (1.0 - sig)))).astype(BF))
        edge_grad[:, cols] = jnp.sum(grad_edge * own_rate[:, cols], axis=0, keepdims=True)

    sweep(slot_sum, grad_table, place_out, get_out, place_in, put_in, WB, TURN_B)

    moves[...] = jnp.zeros_like(moves)

    def push_terms(push):
        high = push.astype(BF).astype(F32)
        return jnp.concatenate([high, push - high, jnp.zeros((TERM - 6, push.shape[1]), F32)], axis=0)

    for start in range(0, edges, step):
        cols = slice(start, start + step)
        terms = push_terms(unit[:, cols] * edge_grad[:, cols])
        src_peer = jnp.bitwise_xor(misc[11:12, cols].astype(jnp.int32), me)
        moves[...] += dot_nt(expand(terms, src_peer, peers).astype(BF), source_hot[:, cols])
        moves[:TERM] -= dot_nt(
            jnp.concatenate([terms, jnp.zeros_like(terms)], axis=0).astype(BF), target_hot[:, cols]
        )[:TERM]
    slot_grad = slot_sum[...].T
    for d in range(peers):
        cols = slice(d * ecap, (d + 1) * ecap)
        grads = part_of(slot_grad, channels, d * ecap, ecap)
        slot_unit, src_node, src_peer, dst_node = slots[d]
        terms = push_terms(slot_unit * jnp.sum(grads * slot_rate[:, cols], axis=0, keepdims=True))
        moves[...] += dot_nt(
            expand(terms, jnp.bitwise_xor(src_peer, me), peers).astype(BF), one_hot(src_node, nodes)
        )
        moves[d * TERM : (d + 1) * TERM] -= dot_nt(
            jnp.concatenate([terms, jnp.zeros_like(terms)], axis=0).astype(BF), one_hot(dst_node, nodes)
        )[:TERM]
    half = nodes // 2
    rows = []
    for d in range(peers):
        place = d * TERM
        both = moves[place : place + 3] + moves[place + 3 : place + 6]
        rows += [both[:, :half], both[:, half:]]
    force_out[...] = jnp.concatenate(rows, axis=0)


def exchange(values, axis, distance):
    count = lax.axis_size(axis)
    return lax.ppermute(values, axis, [(i, i ^ distance) for i in range(count)])


def add_over(values, axis):
    count = lax.axis_size(axis)
    if count <= 4:
        total = values
        for d in sorted(range(1, count), key=lambda d: CHAN_ORDER.find(str(d))):
            total = total + exchange(values, axis, d)
        return total
    for bit in range(count.bit_length() - 1):
        values = values + exchange(values, axis, 1 << bit)
    return values


def shards(
    node_embed,
    edge_embed,
    edge_vector,
    triplet_basis,
    w_source,
    w_target,
    w_edge,
    w_radial,
    w_angle,
    w_energy,
    node_send,
    edge_send,
    edge_target,
    edge_source,
    triplet_in,
    triplet_out,
):
    peers = lax.axis_size("graph")
    channels = w_source.shape[1]
    nodes = node_embed.shape[1]
    edges = edge_embed.shape[1]
    trips = triplet_basis.shape[1]
    ecap = edge_send.shape[2]
    groups = 256 // channels
    slots = peers * ecap
    tables = [GIN_F * groups, GOUT_F * groups, GOUT_B * groups, GIN_B * groups]
    shape = pltpu.VMEM
    params = pltpu.CompilerParams(vmem_limit_bytes=VMEM_LIMIT)

    def far(count):
        return [pl.BlockSpec(memory_space=pltpu.HBM)] * count

    def near(count):
        return [pl.BlockSpec(memory_space=pltpu.VMEM)] * count

    def buffers(arrays):
        return [pltpu.VMEM(a.shape, a.dtype) for a in arrays]

    inputs = [
        node_embed,
        w_source.T,
        w_target.T,
        w_edge.T,
        edge_vector,
        node_send,
        edge_send,
        edge_target.reshape(1, edges),
        edge_source.reshape(1, edges),
        edge_embed,
    ]
    part, misc, target_hot, own_node, own_edge, *sends = pl.pallas_call(
        functools.partial(prep_kernel, peers),
        name="prep",
        in_specs=far(len(inputs)),
        out_specs=near(5 + peers),
        out_shape=[
            shape((channels, edges), F32),
            shape((MISC, edges), F32),
            shape((nodes, edges), BF),
            shape((channels, nodes), BF),
            shape((channels, edges), BF),
        ]
        + [shape((2 * channels + MISC, ecap), BF)] * peers,
        scratch_shapes=buffers(inputs) + [pltpu.SemaphoreType.DMA((13,))],
        compiler_params=params,
    )(*[pltpu.with_memory_space_constraint(a, pltpu.HBM) for a in inputs])
    received = [sends[0]] + [exchange(sends[d], "graph", d) for d in range(1, peers)]
    inputs = [
        edge_vector,
        w_radial.T,
        w_angle,
        w_energy.reshape(1, channels),
        triplet_in.reshape(1, trips),
        triplet_out.reshape(1, trips),
        triplet_basis,
    ]
    local = pl.pallas_call(
        functools.partial(local_kernel, ecap),
        name="local",
        in_specs=near(1) + far(len(inputs)),
        out_specs=near(9),
        out_shape=[
            shape((channels, edges), F32),
            shape((channels, edges), F32),
            shape((3, edges), F32),
            shape((channels, trips), F32),
            shape((1, trips), jnp.int32),
            shape((1, trips), jnp.int32),
            shape((nodes, edges), BF),
            shape((channels, w_radial.shape[0]), BF),
            shape((channels, 1), F32),
        ],
        scratch_shapes=buffers(inputs) + [pltpu.SemaphoreType.DMA((7,))],
        compiler_params=params,
        cost_estimate=pl.CostEstimate(flops=2**30, bytes_accessed=2**23, transcendentals=2**18),
    )(misc, *[pltpu.with_memory_space_constraint(a, pltpu.HBM) for a in inputs])
    node_out, edge_out, force = pl.pallas_call(
        functools.partial(main_kernel, peers, ecap, math.sqrt(NODE_DEV / EDGE_DEV)),
        name="main",
        out_shape=[
            jax.ShapeDtypeStruct((channels, nodes), BF),
            jax.ShapeDtypeStruct((channels, edges), BF),
            shape((peers * 6, nodes // 2), F32),
        ],
        scratch_shapes=[
            pltpu.VMEM((channels, edges), BF),
            pltpu.VMEM((channels, edges), F32),
            pltpu.VMEM((channels, slots), F32),
            pltpu.VMEM((tables[0] * channels, slots // tables[0]), BF),
            pltpu.VMEM((edges // tables[1], tables[1] * channels), F32),
            pltpu.VMEM((tables[2] * channels, edges // tables[2]), BF),
            pltpu.VMEM((1, edges), F32),
            pltpu.VMEM((slots // tables[3], tables[3] * channels), F32),
            pltpu.VMEM((peers * TERM, nodes), F32),
        ],
        compiler_params=params,
    )(part, misc, target_hot, own_node, own_edge, *local, *received)
    mine = force[:6]
    for d in sorted(range(1, peers), key=lambda d: GRAPH_ORDER.find(str(d))):
        mine = mine + exchange(force[6 * d : 6 * d + 6], "graph", d)
    mine = add_over(mine, "chan")
    return node_out, edge_out, jnp.concatenate([mine[:3], mine[3:]], axis=1)


def solution(mesh):
    placed = (
        P(None, ("groups", "graph")),
        P(None, ("groups", "graph")),
        P(None, ("groups", "graph")),
        P(None, ("groups", "graph")),
        P(None, "chan"),
        P(None, "chan"),
        P(None, "chan"),
        P(None, "chan"),
        P(None, "chan"),
        P("chan"),
        P("groups", None, None),
        P("groups", None, None),
        P(("groups", "graph")),
        P(("groups", "graph")),
        P(("groups", "graph")),
        P(("groups", "graph")),
    )
    return jax.shard_map(
        shards,
        mesh=mesh,
        in_specs=placed,
        out_specs=(
            P("chan", ("groups", "graph")),
            P("chan", ("groups", "graph")),
            P(None, ("groups", "graph")),
        ),
        check_vma=False,
    )
```

```python
import functools
import math

import jax
import jax.numpy as jnp
from jax import lax
from jax.experimental import pallas as pl
from jax.experimental.pallas import tpu as pltpu
from jax.sharding import PartitionSpec as P

NODE_DEV = 256
EDGE_DEV = 2048

radius_max = 8.0
MISC = 16
TERM = 8
BF = jnp.bfloat16
F32 = jnp.float32
VMEM_LIMIT = 24 * 1024 * 1024
GRAPH_ORDER, CHAN_ORDER = "213", "123"
GIN_F, GOUT_F, GOUT_B, GIN_B = 1, 2, 1, 1
WF = 2048
WB = 2048
TURN_F = 8192
TURN_B = 8192


def sigmoid(values):
    return 1.0 / (1.0 + jnp.exp(-values))


def dot_tn(weight, data):
    return lax.dot_general(weight, data, (((0,), (0,)), ((), ())), preferred_element_type=F32)


def dot_nn(left, right):
    return lax.dot_general(left, right, (((1,), (0,)), ((), ())), preferred_element_type=F32)


def dot_nt(left, right):
    return lax.dot_general(left, right, (((1,), (1,)), ((), ())), preferred_element_type=F32)


def one_hot(row, count):
    lines = lax.broadcasted_iota(jnp.int16, (count, row.shape[1]), 0)
    one = jnp.ones((count, row.shape[1]), BF)
    return jnp.where(lines == row.astype(jnp.int16), one, jnp.zeros_like(one))


def choose(stacked, group, groups):
    rows = stacked.shape[0] // groups
    out = jnp.where(group == 0, stacked[:rows], 0.0)
    for g in range(1, groups):
        out = jnp.where(group == g, stacked[g * rows : (g + 1) * rows], out)
    return out


def expand(values, group, groups):
    zero = jnp.zeros_like(values)
    return jnp.concatenate([jnp.where(group == g, values, zero) for g in range(groups)], axis=0)


def halves(values):
    high = values.astype(BF)
    return high, (values - high.astype(F32)).astype(BF)


def radial_terms(squared, weight):
    count = weight.shape[1]
    lengths = jnp.sqrt(1.0 + squared)
    spread = 4.0 * radius_max / (count - 1)
    lines = lax.broadcasted_iota(jnp.int32, (count, 1), 0).astype(F32)
    centers = lines * (radius_max / (count - 1))
    offset = (lengths - centers) * (1.0 / spread)
    values = jnp.exp(-offset * offset)
    slopes = values * (offset * (-2.0 / spread))
    return dot_nn(weight, values.astype(BF)), dot_nn(weight, slopes.astype(BF)), lengths


def fetch(sources, places, sems):
    copies = [pltpu.make_async_copy(a, b, sems.at[i]) for i, (a, b) in enumerate(zip(sources, places))]
    for copy in copies:
        copy.start()
    return copies


def squared_length(vector):
    return vector[0:1] * vector[0:1] + vector[1:2] * vector[1:2] + vector[2:3] * vector[2:3]


def prep_kernel(peers, *refs):
    sources = refs[:10]
    part_out, misc_out, target_hot, own_node_out, own_edge_out = refs[10:15]
    sends = refs[15 : 15 + peers]
    places = refs[15 + peers : -1]
    sems = refs[-1]
    edge_source, edge = sources[9], places[9]
    edges = edge.shape[1]
    high_count = 4
    low_count = edges // high_count
    pieces = [slice(h * low_count, (h + 1) * low_count) for h in range(high_count)]
    copies = fetch(
        list(sources[4:9]) + list(sources[:4]) + [edge_source.at[:, cols] for cols in pieces],
        list(places[4:9]) + list(places[:4]) + [edge.at[:, cols] for cols in pieces],
        sems,
    )
    copies = copies[5:9] + copies[:5] + copies[9:]
    node, w_source, w_target, w_edge, vector, node_send, edge_send, target, source = places[:9]
    me = lax.axis_index("graph")
    channels = w_source.shape[0]
    first_chan = pl.multiple_of(lax.axis_index("chan") * channels, channels)
    cap = node_send.shape[2]
    for copy in copies[4:9]:
        copy.wait()
    own_nodes = jnp.concatenate([node_send[q, pl.ds(me, 1), :] for q in range(peers)], axis=0)
    own_nodes = own_nodes.astype(F32).astype(BF)
    miscs = []
    for cols in pieces:
        dst = target[:, cols]
        src = source[:, cols]
        target_hot[:, cols] = one_hot(dst, target_hot.shape[0])
        src_peer = src // cap
        by_peer = dot_nn(own_nodes, one_hot(src - src_peer * cap, cap))
        src_node = choose(by_peer, src_peer, peers)
        vec = vector[:, cols]
        first = vec.astype(BF).astype(F32)
        second = (vec - first).astype(BF).astype(F32)
        third = vec - first - second
        misc = jnp.concatenate(
            [
                first,
                second,
                third,
                dst.astype(F32),
                src_node,
                src_peer.astype(F32),
                jnp.zeros((MISC - 12, low_count), F32),
            ],
            axis=0,
        )
        misc_out[:, cols] = misc
        miscs.append(misc.astype(BF))
    picks = []
    for d in range(peers):
        chosen = edge_send[me, pl.ds(jnp.bitwise_xor(me, d), 1), :]
        high = jnp.where(chosen < 0, -1, chosen // low_count)
        picks.append((high, one_hot(chosen % low_count, low_count)))
    for copy in copies[:4]:
        copy.wait()
    own_node_out[...] = node[pl.ds(first_chan, channels), :]
    atoms = node[...]
    proj_src = dot_nn(w_source[...], atoms).astype(BF)
    dst_high, dst_low = halves(dot_nn(w_target[...], atoms))
    dst_table = jnp.concatenate([dst_high, dst_low], axis=0)
    for d in range(peers):
        sends[d][:channels] = proj_src
    parts = []
    for h, cols in enumerate(pieces):
        rows = dot_nn(dst_table, target_hot[:, cols])
        copies[9 + h].wait()
        part = rows[:channels] + rows[channels:] + dot_nn(w_edge[...], edge[:, cols])
        part_out[:, cols] = part
        own_edge_out[:, cols] = edge[pl.ds(first_chan, channels), cols]
        parts.append(jnp.concatenate([part.astype(BF), miscs[h]], axis=0))
    table = jnp.concatenate(parts, axis=0)
    for d, (high, hot) in enumerate(picks):
        sends[d][channels:] = choose(dot_nn(table, hot), high, high_count).astype(BF)


def local_kernel(ecap, misc, *refs):
    sources = refs[:7]
    radial, rate, unit, angular, place_in, place_out, source_hot, radial_weight, energy_column = refs[7:16]
    places = refs[16:23]
    sems = refs[23]
    copies = fetch(sources, places, sems)
    vector, w_radial, w_angle, w_energy, trip_in, trip_out, basis = places
    me = lax.axis_index("graph")
    edges = vector.shape[1]
    trips = basis.shape[1]
    channels = w_radial.shape[0]
    width = 512
    for start in range(0, edges, width):
        cols = slice(start, start + width)
        source_hot[:, cols] = one_hot(misc[10:11, cols].astype(jnp.int32), source_hot.shape[0])
    for copy in copies:
        copy.wait()
    radial_weight[...] = w_radial[...]
    lines = lax.broadcasted_iota(jnp.int32, (channels, channels), 0)
    diagonal = lines == lax.broadcasted_iota(jnp.int32, (channels, channels), 1)
    energy_column[...] = jnp.sum(jnp.where(diagonal, w_energy[...], 0.0), axis=1, keepdims=True)
    for start in range(0, edges, width):
        cols = slice(start, start + width)
        vec = vector[:, cols]
        rows, slopes, lengths = radial_terms(squared_length(vec), w_radial[...])
        radial[:, cols] = rows
        rate[:, cols] = slopes
        unit[:, cols] = vec / lengths
    for start in range(0, trips, width):
        cols = slice(start, start + width)
        angular[:, cols] = dot_tn(w_angle[...], basis[:, cols])
        place_in[:, cols] = jnp.bitwise_xor(trip_in[:, cols], me * ecap)
        place_out[:, cols] = trip_out[:, cols]


def push_terms(push):
    high = push.astype(BF).astype(F32)
    return jnp.concatenate([high, push - high, jnp.zeros((TERM - 6, push.shape[1]), F32)], axis=0)


def late_kernel(unit, edge_grad, target_hot, out):
    terms = push_terms(unit[...] * edge_grad[...])
    sums = dot_nt(jnp.concatenate([terms, jnp.zeros_like(terms)], axis=0).astype(BF), target_hot[...])
    both = -(sums[:3] + sums[3:6])
    half = both.shape[1] // 2
    out[...] = jnp.concatenate([both[:, :half], both[:, half:]], axis=0)


def keep(table, start, values):
    channels, count = values.shape
    low = table.shape[1]
    piece = min(low, count)
    for at in range(0, count, piece):
        group, off = divmod(start + at, low)
        table[group * channels : (group + 1) * channels, off : off + piece] = values[:, at : at + piece]


def part_of(table, channels, start, count):
    low = table.shape[1]
    piece = min(low, count)
    out = []
    for at in range(start, start + count, piece):
        group, off = divmod(at, low)
        out.append(table[group * channels : (group + 1) * channels, off : off + piece])
    return jnp.concatenate(out, axis=1) if len(out) > 1 else out[0]


def main_kernel(
    peers,
    ecap,
    scale,
    part,
    misc,
    target_hot,
    node,
    edge,
    radial,
    rate,
    unit,
    angular,
    place_in,
    place_out,
    source_hot,
    w_radial,
    w_energy,
    *refs,
):
    received = refs[:peers]
    node_out, edge_out, force_out, edge_grad = refs[peers : peers + 4]
    message, own_rate, slot_rate, slot_table, gather_sum, grad_table, slot_sum, moves = refs[peers + 4 :]
    me = lax.axis_index("graph")
    channels, edges = part.shape
    nodes = node.shape[1]
    trips = angular.shape[1]
    get_in, low_in = slot_table.shape[0] // channels, slot_table.shape[1]
    put_out, low_put = gather_sum.shape[1] // channels, gather_sum.shape[0]
    get_out, low_get = grad_table.shape[0] // channels, grad_table.shape[1]
    put_in, low_back = slot_sum.shape[1] // channels, slot_sum.shape[0]
    step = 256

    src_table = jnp.concatenate([received[d][:channels] for d in range(peers)], axis=0)

    def src_rows(hot, src_peer):
        return choose(dot_nn(src_table, hot), jnp.bitwise_xor(src_peer, me), peers)

    for start in range(0, edges, step):
        cols = slice(start, start + step)
        preact = src_rows(source_hot[:, cols], misc[11:12, cols].astype(jnp.int32)) + part[:, cols]
        active = preact * sigmoid(preact)
        message[:, cols] = (active * radial[:, cols]).astype(BF)
        own_rate[:, cols] = active * rate[:, cols]
    slots = []
    for d in range(peers):
        cols = slice(d * ecap, (d + 1) * ecap)
        extra = received[d][channels:].astype(F32)
        rest = extra[channels:]
        vec = rest[0:3] + rest[3:6] + rest[6:9]
        src_node = rest[10:11].astype(jnp.int32)
        src_peer = rest[11:12].astype(jnp.int32)
        slot_radial, slot_slope, lengths = radial_terms(squared_length(vec), w_radial[...])
        preact = src_rows(one_hot(src_node, nodes), src_peer) + extra[:channels]
        active = preact * sigmoid(preact)
        keep(slot_table, d * ecap, (active * slot_radial).astype(BF))
        slot_rate[:, cols] = active * slot_slope
        slots.append((vec / lengths, src_node, src_peer, rest[9:10].astype(jnp.int32)))

    def split(place, low_count):
        high = place // low_count
        return high, one_hot(place - high * low_count, low_count)

    def sweep(total, table, get_place, get_groups, put_place, put_groups, width, turn_width):
        width, turn_width = min(width, trips), min(turn_width, trips)

        def turn(number):
            found = None
            for sub in range(turn_width // width):
                cols = slice(number * turn_width + sub * width, number * turn_width + (sub + 1) * width)
                high_get, hot_get = split(get_place[:, cols], table.shape[1])
                high_put, hot_put = split(put_place[:, cols], total.shape[0])
                wide = dot_nn(table[...], hot_get)
                rows = wide.shape[0] // get_groups
                picked = wide[:rows]
                for g in range(1, get_groups):
                    picked = jnp.where(high_get == g, wide[g * rows : (g + 1) * rows], picked)
                term = picked * angular[:, cols]
                more = dot_nt(hot_put, expand(term.astype(BF), high_put, put_groups))
                found = more if found is None else found + more
            return found

        total[...] = functools.reduce(jnp.add, [turn(number) for number in range(trips // turn_width)])

    sweep(gather_sum, slot_table, place_in, get_in, place_out, put_out, WF, TURN_F)

    gathered = gather_sum[...].T
    atom_sum = jnp.zeros((channels, nodes), F32)
    for start in range(0, edges, step):
        cols = slice(start, start + step)
        value = part_of(gathered, channels, start, step)
        fresh = edge[:, cols].astype(F32) + message[:, cols].astype(F32) + value * sigmoid(value)
        edge_out[:, cols] = fresh.astype(BF)
        high, low = halves(fresh)
        sums = dot_nt(jnp.concatenate([high, low], axis=0), target_hot[:, cols])
        atom_sum += sums[:channels] + sums[channels:]
    node_new = node[...].astype(F32) + scale * atom_sum
    node_out[...] = node_new.astype(BF)
    sig = sigmoid(node_new)
    grad_node = w_energy[...] * (sig * (1.0 + node_new * (1.0 - sig))) * scale
    high, low = halves(grad_node)
    grad_pair = jnp.concatenate([high, low], axis=0)
    for start in range(0, edges, step):
        cols = slice(start, start + step)
        value = part_of(gathered, channels, start, step)
        rows = dot_nn(grad_pair, target_hot[:, cols])
        grad_edge = rows[:channels] + rows[channels:]
        sig = sigmoid(value)
        keep(grad_table, start, (grad_edge * (sig * (1.0 + value * (1.0 - sig)))).astype(BF))
        edge_grad[:, cols] = jnp.sum(grad_edge * own_rate[:, cols], axis=0, keepdims=True)

    sweep(slot_sum, grad_table, place_out, get_out, place_in, put_in, WB, TURN_B)

    src_peer = jnp.bitwise_xor(misc[11:12, :].astype(jnp.int32), me)
    terms = push_terms(unit[...] * edge_grad[...])
    moves[...] = dot_nt(expand(terms, src_peer, peers).astype(BF), source_hot[...])
    slot_grad = slot_sum[...].T
    for d in range(peers):
        cols = slice(d * ecap, (d + 1) * ecap)
        grads = part_of(slot_grad, channels, d * ecap, ecap)
        slot_unit, src_node, src_peer, dst_node = slots[d]
        terms = push_terms(slot_unit * jnp.sum(grads * slot_rate[:, cols], axis=0, keepdims=True))
        moves[...] += dot_nt(
            expand(terms, jnp.bitwise_xor(src_peer, me), peers).astype(BF), one_hot(src_node, nodes)
        )
        moves[d * TERM : (d + 1) * TERM] -= dot_nt(
            jnp.concatenate([terms, jnp.zeros_like(terms)], axis=0).astype(BF), one_hot(dst_node, nodes)
        )[:TERM]
    half = nodes // 2
    rows = []
    for d in range(peers):
        place = d * TERM
        both = moves[place : place + 3] + moves[place + 3 : place + 6]
        rows += [both[:, :half], both[:, half:]]
    force_out[...] = jnp.concatenate(rows, axis=0)


def exchange(values, axis, distance):
    count = lax.axis_size(axis)
    return lax.ppermute(values, axis, [(i, i ^ distance) for i in range(count)])


def add_over(values, axis):
    count = lax.axis_size(axis)
    if count <= 4:
        total = values
        for d in sorted(range(1, count), key=lambda d: CHAN_ORDER.find(str(d))):
            total = total + exchange(values, axis, d)
        return total
    for bit in range(count.bit_length() - 1):
        values = values + exchange(values, axis, 1 << bit)
    return values


def shards(
    node_embed,
    edge_embed,
    edge_vector,
    triplet_basis,
    w_source,
    w_target,
    w_edge,
    w_radial,
    w_angle,
    w_energy,
    node_send,
    edge_send,
    edge_target,
    edge_source,
    triplet_in,
    triplet_out,
):
    peers = lax.axis_size("graph")
    channels = w_source.shape[1]
    nodes = node_embed.shape[1]
    edges = edge_embed.shape[1]
    trips = triplet_basis.shape[1]
    ecap = edge_send.shape[2]
    groups = 256 // channels
    slots = peers * ecap
    tables = [GIN_F * groups, GOUT_F * groups, GOUT_B * groups, GIN_B * groups]
    shape = pltpu.VMEM
    params = pltpu.CompilerParams(vmem_limit_bytes=VMEM_LIMIT)

    def far(count):
        return [pl.BlockSpec(memory_space=pltpu.HBM)] * count

    def near(count):
        return [pl.BlockSpec(memory_space=pltpu.VMEM)] * count

    def buffers(arrays):
        return [pltpu.VMEM(a.shape, a.dtype) for a in arrays]

    inputs = [
        node_embed,
        w_source.T,
        w_target.T,
        w_edge.T,
        edge_vector,
        node_send,
        edge_send,
        edge_target.reshape(1, edges),
        edge_source.reshape(1, edges),
        edge_embed,
    ]
    part, misc, target_hot, own_node, own_edge, *sends = pl.pallas_call(
        functools.partial(prep_kernel, peers),
        name="prep",
        in_specs=far(len(inputs)),
        out_specs=near(5 + peers),
        out_shape=[
            shape((channels, edges), F32),
            shape((MISC, edges), F32),
            shape((nodes, edges), BF),
            shape((channels, nodes), BF),
            shape((channels, edges), BF),
        ]
        + [shape((2 * channels + MISC, ecap), BF)] * peers,
        scratch_shapes=buffers(inputs) + [pltpu.SemaphoreType.DMA((13,))],
        compiler_params=params,
    )(*[pltpu.with_memory_space_constraint(a, pltpu.HBM) for a in inputs])
    received = [sends[0]] + [exchange(sends[d], "graph", d) for d in range(1, peers)]
    inputs = [
        edge_vector,
        w_radial.T,
        w_angle,
        w_energy.reshape(1, channels),
        triplet_in.reshape(1, trips),
        triplet_out.reshape(1, trips),
        triplet_basis,
    ]
    local = pl.pallas_call(
        functools.partial(local_kernel, ecap),
        name="local",
        in_specs=near(1) + far(len(inputs)),
        out_specs=near(9),
        out_shape=[
            shape((channels, edges), F32),
            shape((channels, edges), F32),
            shape((3, edges), F32),
            shape((channels, trips), F32),
            shape((1, trips), jnp.int32),
            shape((1, trips), jnp.int32),
            shape((nodes, edges), BF),
            shape((channels, w_radial.shape[0]), BF),
            shape((channels, 1), F32),
        ],
        scratch_shapes=buffers(inputs) + [pltpu.SemaphoreType.DMA((7,))],
        compiler_params=params,
        cost_estimate=pl.CostEstimate(flops=2**30, bytes_accessed=2**23, transcendentals=2**18),
    )(misc, *[pltpu.with_memory_space_constraint(a, pltpu.HBM) for a in inputs])
    node_out, edge_out, force, edge_grad = pl.pallas_call(
        functools.partial(main_kernel, peers, ecap, math.sqrt(NODE_DEV / EDGE_DEV)),
        name="main",
        out_shape=[
            jax.ShapeDtypeStruct((channels, nodes), BF),
            jax.ShapeDtypeStruct((channels, edges), BF),
            shape((peers * 6, nodes // 2), F32),
            shape((1, edges), F32),
        ],
        scratch_shapes=[
            pltpu.VMEM((channels, edges), BF),
            pltpu.VMEM((channels, edges), F32),
            pltpu.VMEM((channels, slots), F32),
            pltpu.VMEM((tables[0] * channels, slots // tables[0]), BF),
            pltpu.VMEM((edges // tables[1], tables[1] * channels), F32),
            pltpu.VMEM((tables[2] * channels, edges // tables[2]), BF),
            pltpu.VMEM((slots // tables[3], tables[3] * channels), F32),
            pltpu.VMEM((peers * TERM, nodes), F32),
        ],
        compiler_params=params,
    )(part, misc, target_hot, own_node, own_edge, *local, *received)
    unit = local[2]
    late = pl.pallas_call(
        late_kernel,
        name="late",
        out_shape=shape((6, nodes // 2), F32),
        compiler_params=params,
        cost_estimate=pl.CostEstimate(flops=2**28, bytes_accessed=2**21, transcendentals=0),
    )(unit, edge_grad, target_hot)
    mine = force[:6] + late
    for d in sorted(range(1, peers), key=lambda d: GRAPH_ORDER.find(str(d))):
        mine = mine + exchange(force[6 * d : 6 * d + 6], "graph", d)
    mine = add_over(mine, "chan")
    return node_out, edge_out, jnp.concatenate([mine[:3], mine[3:]], axis=1)


def solution(mesh):
    placed = (
        P(None, ("groups", "graph")),
        P(None, ("groups", "graph")),
        P(None, ("groups", "graph")),
        P(None, ("groups", "graph")),
        P(None, "chan"),
        P(None, "chan"),
        P(None, "chan"),
        P(None, "chan"),
        P(None, "chan"),
        P("chan"),
        P("groups", None, None),
        P("groups", None, None),
        P(("groups", "graph")),
        P(("groups", "graph")),
        P(("groups", "graph")),
        P(("groups", "graph")),
    )
    return jax.shard_map(
        shards,
        mesh=mesh,
        in_specs=placed,
        out_specs=(
            P("chan", ("groups", "graph")),
            P("chan", ("groups", "graph")),
            P(None, ("groups", "graph")),
        ),
        check_vma=False,
    )
```

```python
import functools
import math

import jax
import jax.numpy as jnp
from jax import lax
from jax.experimental import pallas as pl
from jax.experimental.pallas import tpu as pltpu
from jax.sharding import PartitionSpec as P

NODE_DEV = 256
EDGE_DEV = 2048

radius_max = 8.0
MISC = 16
TERM = 8
BF = jnp.bfloat16
F32 = jnp.float32
VMEM_LIMIT = 24 * 1024 * 1024
GRAPH_ORDER, CHAN_ORDER = "213", "132"
GIN_F, GOUT_F, GOUT_B, GIN_B = 1, 2, 1, 1
WF = 2048
WB = 2048
TURN_F = 8192
TURN_B = 8192


def sigmoid(values):
    return 1.0 / (1.0 + jnp.exp(-values))


def dot_tn(weight, data):
    return lax.dot_general(weight, data, (((0,), (0,)), ((), ())), preferred_element_type=F32)


def dot_nn(left, right):
    return lax.dot_general(left, right, (((1,), (0,)), ((), ())), preferred_element_type=F32)


def dot_nt(left, right):
    return lax.dot_general(left, right, (((1,), (1,)), ((), ())), preferred_element_type=F32)


def one_hot(row, count):
    lines = lax.broadcasted_iota(jnp.int16, (count, row.shape[1]), 0)
    one = jnp.ones((count, row.shape[1]), BF)
    return jnp.where(lines == row.astype(jnp.int16), one, jnp.zeros_like(one))


def choose(stacked, group, groups):
    rows = stacked.shape[0] // groups
    out = jnp.where(group == 0, stacked[:rows], 0.0)
    for g in range(1, groups):
        out = jnp.where(group == g, stacked[g * rows : (g + 1) * rows], out)
    return out


def expand(values, group, groups):
    zero = jnp.zeros_like(values)
    return jnp.concatenate([jnp.where(group == g, values, zero) for g in range(groups)], axis=0)


def halves(values):
    high = values.astype(BF)
    return high, (values - high.astype(F32)).astype(BF)


def radial_terms(squared, weight):
    count = weight.shape[1]
    lengths = jnp.sqrt(1.0 + squared)
    spread = 4.0 * radius_max / (count - 1)
    lines = lax.broadcasted_iota(jnp.int32, (count, 1), 0).astype(F32)
    centers = lines * (radius_max / (count - 1))
    offset = (lengths - centers) * (1.0 / spread)
    values = jnp.exp(-offset * offset)
    slopes = values * (offset * (-2.0 / spread))
    return dot_nn(weight, values.astype(BF)), dot_nn(weight, slopes.astype(BF)), lengths


def fetch(sources, places, sems):
    copies = [pltpu.make_async_copy(a, b, sems.at[i]) for i, (a, b) in enumerate(zip(sources, places))]
    for copy in copies:
        copy.start()
    return copies


def squared_length(vector):
    return vector[0:1] * vector[0:1] + vector[1:2] * vector[1:2] + vector[2:3] * vector[2:3]


def prep_kernel(peers, *refs):
    sources = refs[:10]
    part_out, misc_out, target_hot, own_node_out, own_edge_out = refs[10:15]
    sends = refs[15 : 15 + peers]
    places = refs[15 + peers : -1]
    sems = refs[-1]
    edge_source, edge = sources[9], places[9]
    edges = edge.shape[1]
    high_count = 4
    low_count = edges // high_count
    pieces = [slice(h * low_count, (h + 1) * low_count) for h in range(high_count)]
    copies = fetch(
        list(sources[4:9]) + list(sources[:4]) + [edge_source.at[:, cols] for cols in pieces],
        list(places[4:9]) + list(places[:4]) + [edge.at[:, cols] for cols in pieces],
        sems,
    )
    copies = copies[5:9] + copies[:5] + copies[9:]
    node, w_source, w_target, w_edge, vector, node_send, edge_send, target, source = places[:9]
    me = lax.axis_index("graph")
    channels = w_source.shape[0]
    first_chan = pl.multiple_of(lax.axis_index("chan") * channels, channels)
    cap = node_send.shape[2]
    for copy in copies[4:9]:
        copy.wait()
    own_nodes = jnp.concatenate([node_send[q, pl.ds(me, 1), :] for q in range(peers)], axis=0)
    own_nodes = own_nodes.astype(F32).astype(BF)
    miscs = []
    for cols in pieces:
        dst = target[:, cols]
        src = source[:, cols]
        target_hot[:, cols] = one_hot(dst, target_hot.shape[0])
        src_peer = src // cap
        by_peer = dot_nn(own_nodes, one_hot(src - src_peer * cap, cap))
        src_node = choose(by_peer, src_peer, peers)
        vec = vector[:, cols]
        first = vec.astype(BF).astype(F32)
        second = (vec - first).astype(BF).astype(F32)
        third = vec - first - second
        misc = jnp.concatenate(
            [
                first,
                second,
                third,
                dst.astype(F32),
                src_node,
                src_peer.astype(F32),
                jnp.zeros((MISC - 12, low_count), F32),
            ],
            axis=0,
        )
        misc_out[:, cols] = misc
        miscs.append(misc.astype(BF))
    picks = []
    for d in range(peers):
        chosen = edge_send[me, pl.ds(jnp.bitwise_xor(me, d), 1), :]
        high = jnp.where(chosen < 0, -1, chosen // low_count)
        picks.append((high, one_hot(chosen % low_count, low_count)))
    for copy in copies[:4]:
        copy.wait()
    own_node_out[...] = node[pl.ds(first_chan, channels), :]
    atoms = node[...]
    proj_src = dot_nn(w_source[...], atoms).astype(BF)
    dst_high, dst_low = halves(dot_nn(w_target[...], atoms))
    dst_table = jnp.concatenate([dst_high, dst_low], axis=0)
    for d in range(peers):
        sends[d][:channels] = proj_src
    parts = []
    for h, cols in enumerate(pieces):
        rows = dot_nn(dst_table, target_hot[:, cols])
        copies[9 + h].wait()
        part = rows[:channels] + rows[channels:] + dot_nn(w_edge[...], edge[:, cols])
        part_out[:, cols] = part
        own_edge_out[:, cols] = edge[pl.ds(first_chan, channels), cols]
        parts.append(jnp.concatenate([part.astype(BF), miscs[h]], axis=0))
    table = jnp.concatenate(parts, axis=0)
    for d, (high, hot) in enumerate(picks):
        sends[d][channels:] = choose(dot_nn(table, hot), high, high_count).astype(BF)


def local_kernel(ecap, misc, *refs):
    sources = refs[:7]
    radial, rate, unit, angular, place_in, place_out, source_hot, radial_weight, energy_column = refs[7:16]
    places = refs[16:23]
    sems = refs[23]
    copies = fetch(sources, places, sems)
    vector, w_radial, w_angle, w_energy, trip_in, trip_out, basis = places
    me = lax.axis_index("graph")
    edges = vector.shape[1]
    trips = basis.shape[1]
    channels = w_radial.shape[0]
    width = 512
    for start in range(0, edges, width):
        cols = slice(start, start + width)
        source_hot[:, cols] = one_hot(misc[10:11, cols].astype(jnp.int32), source_hot.shape[0])
    for copy in copies:
        copy.wait()
    radial_weight[...] = w_radial[...]
    lines = lax.broadcasted_iota(jnp.int32, (channels, channels), 0)
    diagonal = lines == lax.broadcasted_iota(jnp.int32, (channels, channels), 1)
    energy_column[...] = jnp.sum(jnp.where(diagonal, w_energy[...], 0.0), axis=1, keepdims=True)
    for start in range(0, edges, width):
        cols = slice(start, start + width)
        vec = vector[:, cols]
        rows, slopes, lengths = radial_terms(squared_length(vec), w_radial[...])
        radial[:, cols] = rows
        rate[:, cols] = slopes
        unit[:, cols] = vec / lengths
    for start in range(0, trips, width):
        cols = slice(start, start + width)
        angular[:, cols] = dot_tn(w_angle[...], basis[:, cols])
        place_in[:, cols] = jnp.bitwise_xor(trip_in[:, cols], me * ecap)
        place_out[:, cols] = trip_out[:, cols]


def push_terms(push):
    high = push.astype(BF).astype(F32)
    return jnp.concatenate([high, push - high, jnp.zeros((TERM - 6, push.shape[1]), F32)], axis=0)


def late_kernel(unit, edge_grad, target_hot, out):
    terms = push_terms(unit[...] * edge_grad[...])
    sums = dot_nt(jnp.concatenate([terms, jnp.zeros_like(terms)], axis=0).astype(BF), target_hot[...])
    both = -(sums[:3] + sums[3:6])
    half = both.shape[1] // 2
    out[...] = jnp.concatenate([both[:, :half], both[:, half:]], axis=0)


def keep(table, start, values):
    channels, count = values.shape
    low = table.shape[1]
    piece = min(low, count)
    for at in range(0, count, piece):
        group, off = divmod(start + at, low)
        table[group * channels : (group + 1) * channels, off : off + piece] = values[:, at : at + piece]


def part_of(table, channels, start, count):
    low = table.shape[1]
    piece = min(low, count)
    out = []
    for at in range(start, start + count, piece):
        group, off = divmod(at, low)
        out.append(table[group * channels : (group + 1) * channels, off : off + piece])
    return jnp.concatenate(out, axis=1) if len(out) > 1 else out[0]


def main_kernel(
    peers,
    ecap,
    scale,
    part,
    misc,
    target_hot,
    node,
    edge,
    radial,
    rate,
    unit,
    angular,
    place_in,
    place_out,
    source_hot,
    w_radial,
    w_energy,
    *refs,
):
    received = refs[:peers]
    node_out, edge_out, force_out, edge_grad = refs[peers : peers + 4]
    message, own_rate, slot_rate, slot_table, gather_sum, grad_table, slot_sum, moves = refs[peers + 4 :]
    me = lax.axis_index("graph")
    channels, edges = part.shape
    nodes = node.shape[1]
    trips = angular.shape[1]
    get_in, low_in = slot_table.shape[0] // channels, slot_table.shape[1]
    put_out, low_put = gather_sum.shape[1] // channels, gather_sum.shape[0]
    get_out, low_get = grad_table.shape[0] // channels, grad_table.shape[1]
    put_in, low_back = slot_sum.shape[1] // channels, slot_sum.shape[0]
    step = 256

    src_table = jnp.concatenate([received[d][:channels] for d in range(peers)], axis=0)

    def src_rows(hot, src_peer):
        return choose(dot_nn(src_table, hot), jnp.bitwise_xor(src_peer, me), peers)

    for start in range(0, edges, step):
        cols = slice(start, start + step)
        preact = src_rows(source_hot[:, cols], misc[11:12, cols].astype(jnp.int32)) + part[:, cols]
        active = preact * sigmoid(preact)
        message[:, cols] = (active * radial[:, cols]).astype(BF)
        own_rate[:, cols] = active * rate[:, cols]
    slots = []
    for d in range(peers):
        cols = slice(d * ecap, (d + 1) * ecap)
        extra = received[d][channels:].astype(F32)
        rest = extra[channels:]
        vec = rest[0:3] + rest[3:6] + rest[6:9]
        src_node = rest[10:11].astype(jnp.int32)
        src_peer = rest[11:12].astype(jnp.int32)
        slot_radial, slot_slope, lengths = radial_terms(squared_length(vec), w_radial[...])
        preact = src_rows(one_hot(src_node, nodes), src_peer) + extra[:channels]
        active = preact * sigmoid(preact)
        keep(slot_table, d * ecap, (active * slot_radial).astype(BF))
        slot_rate[:, cols] = active * slot_slope
        slots.append((vec / lengths, src_node, src_peer, rest[9:10].astype(jnp.int32)))

    def split(place, low_count):
        high = place // low_count
        return high, one_hot(place - high * low_count, low_count)

    def sweep(total, table, get_place, get_groups, put_place, put_groups, width, turn_width):
        width, turn_width = min(width, trips), min(turn_width, trips)

        def turn(number):
            found = None
            for sub in range(turn_width // width):
                cols = slice(number * turn_width + sub * width, number * turn_width + (sub + 1) * width)
                high_get, hot_get = split(get_place[:, cols], table.shape[1])
                high_put, hot_put = split(put_place[:, cols], total.shape[0])
                wide = dot_nn(table[...], hot_get)
                rows = wide.shape[0] // get_groups
                picked = wide[:rows]
                for g in range(1, get_groups):
                    picked = jnp.where(high_get == g, wide[g * rows : (g + 1) * rows], picked)
                term = picked * angular[:, cols]
                more = dot_nt(hot_put, expand(term.astype(BF), high_put, put_groups))
                found = more if found is None else found + more
            return found

        total[...] = functools.reduce(jnp.add, [turn(number) for number in range(trips // turn_width)])

    sweep(gather_sum, slot_table, place_in, get_in, place_out, put_out, WF, TURN_F)

    gathered = gather_sum[...].T
    atom_sum = jnp.zeros((channels, nodes), F32)
    for start in range(0, edges, step):
        cols = slice(start, start + step)
        value = part_of(gathered, channels, start, step)
        fresh = edge[:, cols].astype(F32) + message[:, cols].astype(F32) + value * sigmoid(value)
        edge_out[:, cols] = fresh.astype(BF)
        high, low = halves(fresh)
        sums = dot_nt(jnp.concatenate([high, low], axis=0), target_hot[:, cols])
        atom_sum += sums[:channels] + sums[channels:]
    node_new = node[...].astype(F32) + scale * atom_sum
    node_out[...] = node_new.astype(BF)
    sig = sigmoid(node_new)
    grad_node = w_energy[...] * (sig * (1.0 + node_new * (1.0 - sig))) * scale
    high, low = halves(grad_node)
    grad_pair = jnp.concatenate([high, low], axis=0)
    for start in range(0, edges, step):
        cols = slice(start, start + step)
        value = part_of(gathered, channels, start, step)
        rows = dot_nn(grad_pair, target_hot[:, cols])
        grad_edge = rows[:channels] + rows[channels:]
        sig = sigmoid(value)
        keep(grad_table, start, (grad_edge * (sig * (1.0 + value * (1.0 - sig)))).astype(BF))
        edge_grad[:, cols] = jnp.sum(grad_edge * own_rate[:, cols], axis=0, keepdims=True)

    sweep(slot_sum, grad_table, place_out, get_out, place_in, put_in, WB, TURN_B)

    src_peer = jnp.bitwise_xor(misc[11:12, :].astype(jnp.int32), me)
    terms = push_terms(unit[...] * edge_grad[...])
    moves[...] = dot_nt(expand(terms, src_peer, peers).astype(BF), source_hot[...])
    slot_grad = slot_sum[...].T
    for d in range(peers):
        cols = slice(d * ecap, (d + 1) * ecap)
        grads = part_of(slot_grad, channels, d * ecap, ecap)
        slot_unit, src_node, src_peer, dst_node = slots[d]
        terms = push_terms(slot_unit * jnp.sum(grads * slot_rate[:, cols], axis=0, keepdims=True))
        moves[...] += dot_nt(
            expand(terms, jnp.bitwise_xor(src_peer, me), peers).astype(BF), one_hot(src_node, nodes)
        )
        moves[d * TERM : (d + 1) * TERM] -= dot_nt(
            jnp.concatenate([terms, jnp.zeros_like(terms)], axis=0).astype(BF), one_hot(dst_node, nodes)
        )[:TERM]
    half = nodes // 2
    rows = []
    for d in range(peers):
        place = d * TERM
        both = moves[place : place + 3] + moves[place + 3 : place + 6]
        rows += [both[:, :half], both[:, half:]]
    force_out[...] = jnp.concatenate(rows, axis=0)


def exchange(values, axis, distance):
    count = lax.axis_size(axis)
    return lax.ppermute(values, axis, [(i, i ^ distance) for i in range(count)])


def add_over(values, axis):
    count = lax.axis_size(axis)
    if count <= 4:
        total = values
        for d in sorted(range(1, count), key=lambda d: CHAN_ORDER.find(str(d))):
            total = total + exchange(values, axis, d)
        return total
    for bit in range(count.bit_length() - 1):
        values = values + exchange(values, axis, 1 << bit)
    return values


def shards(
    node_embed,
    edge_embed,
    edge_vector,
    triplet_basis,
    w_source,
    w_target,
    w_edge,
    w_radial,
    w_angle,
    w_energy,
    node_send,
    edge_send,
    edge_target,
    edge_source,
    triplet_in,
    triplet_out,
):
    peers = lax.axis_size("graph")
    channels = w_source.shape[1]
    nodes = node_embed.shape[1]
    edges = edge_embed.shape[1]
    trips = triplet_basis.shape[1]
    ecap = edge_send.shape[2]
    groups = 256 // channels
    slots = peers * ecap
    tables = [GIN_F * groups, GOUT_F * groups, GOUT_B * groups, GIN_B * groups]
    shape = pltpu.VMEM
    params = pltpu.CompilerParams(vmem_limit_bytes=VMEM_LIMIT)

    def far(count):
        return [pl.BlockSpec(memory_space=pltpu.HBM)] * count

    def near(count):
        return [pl.BlockSpec(memory_space=pltpu.VMEM)] * count

    def buffers(arrays):
        return [pltpu.VMEM(a.shape, a.dtype) for a in arrays]

    inputs = [
        node_embed,
        w_source.T,
        w_target.T,
        w_edge.T,
        edge_vector,
        node_send,
        edge_send,
        edge_target.reshape(1, edges),
        edge_source.reshape(1, edges),
        edge_embed,
    ]
    part, misc, target_hot, own_node, own_edge, *sends = pl.pallas_call(
        functools.partial(prep_kernel, peers),
        name="prep",
        in_specs=far(len(inputs)),
        out_specs=near(5 + peers),
        out_shape=[
            shape((channels, edges), F32),
            shape((MISC, edges), F32),
            shape((nodes, edges), BF),
            shape((channels, nodes), BF),
            shape((channels, edges), BF),
        ]
        + [shape((2 * channels + MISC, ecap), BF)] * peers,
        scratch_shapes=buffers(inputs) + [pltpu.SemaphoreType.DMA((13,))],
        compiler_params=params,
    )(*[pltpu.with_memory_space_constraint(a, pltpu.HBM) for a in inputs])
    received = [sends[0]] + [exchange(sends[d], "graph", d) for d in range(1, peers)]
    inputs = [
        edge_vector,
        w_radial.T,
        w_angle,
        w_energy.reshape(1, channels),
        triplet_in.reshape(1, trips),
        triplet_out.reshape(1, trips),
        triplet_basis,
    ]
    local = pl.pallas_call(
        functools.partial(local_kernel, ecap),
        name="local",
        in_specs=near(1) + far(len(inputs)),
        out_specs=near(9),
        out_shape=[
            shape((channels, edges), F32),
            shape((channels, edges), F32),
            shape((3, edges), F32),
            shape((channels, trips), F32),
            shape((1, trips), jnp.int32),
            shape((1, trips), jnp.int32),
            shape((nodes, edges), BF),
            shape((channels, w_radial.shape[0]), BF),
            shape((channels, 1), F32),
        ],
        scratch_shapes=buffers(inputs) + [pltpu.SemaphoreType.DMA((7,))],
        compiler_params=params,
        cost_estimate=pl.CostEstimate(flops=2**30, bytes_accessed=2**23, transcendentals=2**18),
    )(misc, *[pltpu.with_memory_space_constraint(a, pltpu.HBM) for a in inputs])
    node_out, edge_out, force, edge_grad = pl.pallas_call(
        functools.partial(main_kernel, peers, ecap, math.sqrt(NODE_DEV / EDGE_DEV)),
        name="main",
        out_shape=[
            jax.ShapeDtypeStruct((channels, nodes), BF),
            jax.ShapeDtypeStruct((channels, edges), BF),
            shape((peers * 6, nodes // 2), F32),
            shape((1, edges), F32),
        ],
        scratch_shapes=[
            pltpu.VMEM((channels, edges), BF),
            pltpu.VMEM((channels, edges), F32),
            pltpu.VMEM((channels, slots), F32),
            pltpu.VMEM((tables[0] * channels, slots // tables[0]), BF),
            pltpu.VMEM((edges // tables[1], tables[1] * channels), F32),
            pltpu.VMEM((tables[2] * channels, edges // tables[2]), BF),
            pltpu.VMEM((slots // tables[3], tables[3] * channels), F32),
            pltpu.VMEM((peers * TERM, nodes), F32),
        ],
        compiler_params=params,
    )(part, misc, target_hot, own_node, own_edge, *local, *received)
    unit = local[2]
    late = pl.pallas_call(
        late_kernel,
        name="late",
        out_shape=shape((6, nodes // 2), F32),
        compiler_params=params,
        cost_estimate=pl.CostEstimate(flops=2**28, bytes_accessed=2**21, transcendentals=0),
    )(unit, edge_grad, target_hot)
    mine = force[:6] + late
    for d in sorted(range(1, peers), key=lambda d: GRAPH_ORDER.find(str(d))):
        mine = mine + exchange(force[6 * d : 6 * d + 6], "graph", d)
    mine = add_over(mine, "chan")
    return node_out, edge_out, jnp.concatenate([mine[:3], mine[3:]], axis=1)


def solution(mesh):
    placed = (
        P(None, ("groups", "graph")),
        P(None, ("groups", "graph")),
        P(None, ("groups", "graph")),
        P(None, ("groups", "graph")),
        P(None, "chan"),
        P(None, "chan"),
        P(None, "chan"),
        P(None, "chan"),
        P(None, "chan"),
        P("chan"),
        P("groups", None, None),
        P("groups", None, None),
        P(("groups", "graph")),
        P(("groups", "graph")),
        P(("groups", "graph")),
        P(("groups", "graph")),
    )
    return jax.shard_map(
        shards,
        mesh=mesh,
        in_specs=placed,
        out_specs=(
            P("chan", ("groups", "graph")),
            P("chan", ("groups", "graph")),
            P(None, ("groups", "graph")),
        ),
        check_vma=False,
    )
```
